512 devices in a mesh: layer: 16 (over y, core), grid: 32 (over x, z).
Axes of the slice: x: 4, y: 8, z: 8, core: 2. Of those that a mesh axis runs over, the one named last changes fastest.
Arguments:
- l_panels: bfloat16 [16, 2, 8192, 512], P('layer', None, 'grid'), may hold values from -6 to 6
- u_panels: bfloat16 [16, 2, 512, 2048], P('layer', None, 'grid'), may hold values from -0.046875 to 0.046875
- panel_fill: int32 [16, 2, 64, 4], P('layer', None, 'grid'), may hold values 0 or 1
- copy_fill: int32 [16, 64, 16], P('layer', 'grid'), may hold values 0 or 1
- sep_panels: bfloat16 [15, 8192, 256], P(None, 'grid'), may hold values from -0.25 to 0.25
- sep_owner: int32 [15], replicated, may hold values from 0 to 31
Outputs:
- schur: float32 [8192, 2048], P('grid', 'layer')
The draws below stay inside these ranges and needn't reach their ends.
All inputs are finite; a program needn't handle non-finite values. No bound on the sum of `panel_fill` or of `copy_fill` on one device may be relied on, other than what follows from the above.
Results may differ from the reference program's by a relative error of at most 0.0035.
Values may be sent and summed in bfloat16 or wider, within the bound.
A program may use at most 64 MiB of HBM per device.

```python
import jax
import jax.numpy as jnp
from jax import lax

BLOCK = 128
S = 8192
W = 512
WS = 256
PANELS = 2
C = 2048
NODES = 15
N_LAYER = 16
N_GRID = 32


def with_ends(drawn, key, low, largest):
    longest = drawn.shape.index(max(drawn.shape))
    spots = []
    for shift in (0, 1):
        where = [jax.random.randint(jax.random.fold_in(key, axis), (), 0, length) for axis, length in enumerate(drawn.shape)]
        where[longest] = (where[longest] + shift) % drawn.shape[longest]
        spots.append(tuple(where))
    return drawn.at[spots[0]].set(low).at[spots[1]].set(largest)


def steps_of(stream_key, dims, split, smallest, top_value):
    gain, own = 1.0, jax.random.fold_in(stream_key, 6)
    for position, shards_of in split:
        steps = jnp.exp(jax.random.uniform(jax.random.fold_in(own, position), (shards_of,), jnp.float32, smallest / len(split), top_value / len(split)))
        gain = gain * jnp.repeat(steps, dims[position] // shards_of).reshape([-1 if axis == position else 1 for axis in range(len(dims))])
    return gain


def centred(stream_key, shape, spread, bound, split=(), dtype=jnp.bfloat16):
    gain = steps_of(stream_key, shape, split, -0.22, 0.18) if split else 1.0
    array = jax.random.normal(stream_key, shape, jnp.float32) * spread * gain
    return jnp.minimum(jnp.maximum(array, -bound), bound).astype(dtype)


def setup_inputs(seed: int = 0) -> dict:
    key_list = jax.random.split(jax.random.key(seed), 7)
    return {
        "l_panels": centred(key_list[0], (N_LAYER, PANELS, S, W), 1.0, 6.0, ((0, 16), (2, 32))),
        "u_panels": centred(key_list[1], (N_LAYER, PANELS, W, C), (16 * PANELS * W) ** -0.5, 0.046875, ((0, 16), (2, 32))),
        "panel_fill": with_ends((jax.random.randint(key_list[2], (N_LAYER, PANELS, S // BLOCK, W // BLOCK), 0, 4) < 3).astype(jnp.int32), jax.random.fold_in(key_list[2], 1), 0, 1),
        "copy_fill": with_ends((jax.random.randint(key_list[3], (N_LAYER, S // BLOCK, C // BLOCK), 0, 4) < 3).astype(jnp.int32), jax.random.fold_in(key_list[3], 1), 0, 1),
        "sep_panels": centred(key_list[4], (NODES, S, WS), (2 * WS) ** -0.5, 0.25, ((1, 32),)),
        "sep_owner": with_ends(jax.random.randint(key_list[5], (NODES,), 0, N_GRID), jax.random.fold_in(key_list[5], 1), 0, N_GRID - 1).astype(jnp.int32),
    }


def reference(l_panels, u_panels, panel_fill, copy_fill, sep_panels, sep_owner):
    row_count = S // N_GRID

    def layer_copy(layer_id):
        fill_panel = panel_fill[layer_id].astype(jnp.bfloat16)
        masked = (l_panels[layer_id].reshape(PANELS, S // BLOCK, BLOCK, W // BLOCK, BLOCK) * fill_panel[:, :, None, :, None]).reshape(PANELS, S, W)
        left_panel = jnp.concatenate([masked[k] for k in range(PANELS)], axis=1)
        right_panel = u_panels[layer_id].reshape(PANELS * W, C)
        update = jnp.dot(left_panel, right_panel, preferred_element_type=jnp.float32)
        fill_copy = copy_fill[layer_id].astype(jnp.float32)
        return -(update.reshape(S // BLOCK, BLOCK, C // BLOCK, BLOCK) * fill_copy[:, None, :, None]).reshape(S, C)

    def combine(low_layer, group_size):
        if group_size == 1:
            return layer_copy(low_layer)
        half_size = group_size // 2
        combined = combine(low_layer, half_size) + combine(low_layer + half_size, half_size)
        level_index = half_size.bit_length() - 1
        node_index = N_LAYER - (N_LAYER >> level_index) + low_layer // group_size
        owner_index = sep_owner[node_index].astype(jnp.int32)
        pivot_rows = lax.dynamic_slice_in_dim(combined, owner_index * row_count, WS, 0).astype(jnp.bfloat16)
        return combined - jnp.dot(sep_panels[node_index], pivot_rows, preferred_element_type=jnp.float32)

    return combine(0, N_LAYER)
```

```python
import jax
import jax.numpy as jnp
from jax import lax
from jax.sharding import PartitionSpec as P

BLOCK = 128


def from_partner(x, axis, apart):
    return lax.ppermute(x, axis, [(i, i ^ 1 << apart) for i in range(lax.axis_size(axis))])


def spread(x, axis, root):
    mine = lax.axis_index(axis) == root
    return lax.psum(jnp.where(mine, x, jnp.zeros_like(x)), axis)


def reorder(x, count):
    bits = count.bit_length() - 1
    lead = x.ndim - 1
    split = x.reshape(*x.shape[:-1], *(2,) * bits, x.shape[-1] // count)
    axes = [*range(lead), *reversed(range(lead, lead + bits)), lead + bits]
    return split.transpose(axes).reshape(x.shape)


def local(l_panels, u_panels, panel_fill, copy_fill, sep_panels, sep_owner):
    panel_count = l_panels.shape[1]
    row_count = l_panels.shape[2]
    panel_width = l_panels.shape[3]
    columns = u_panels.shape[3]
    layers = lax.axis_size("layer")
    level_count = layers.bit_length() - 1
    layer_index = lax.axis_index("layer")
    u_panels = reorder(u_panels, layers)
    copy_fill = reorder(copy_fill, layers)
    fill_panel = panel_fill[0].astype(jnp.bfloat16)
    masked = (
        l_panels[0].reshape(panel_count, row_count // BLOCK, BLOCK, panel_width // BLOCK, BLOCK)
        * fill_panel[:, :, None, :, None]
    ).reshape(panel_count, row_count, panel_width)
    running = jnp.zeros((row_count, columns), jnp.float32)
    piece = lax.all_gather(u_panels, "grid", axis=2, tiled=True)
    for k in range(panel_count):
        column_part = masked[k]
        running = running + jnp.dot(column_part, piece[0, k], preferred_element_type=jnp.float32)
    fill_copy = copy_fill[0].astype(jnp.float32)
    layer_copy = -(
        running.reshape(row_count // BLOCK, BLOCK, columns // BLOCK, BLOCK)
        * fill_copy[:, None, :, None]
    ).reshape(row_count, columns)
    combined = layer_copy
    for level_index in range(level_count):
        half = combined.shape[1] // 2
        bit = layer_index >> level_index & 1
        keep = lax.dynamic_slice_in_dim(combined, bit * half, half, 1)
        give = lax.dynamic_slice_in_dim(combined, (1 - bit) * half, half, 1)
        wire = jnp.float32 if level_index < 2 else jnp.bfloat16
        combined = keep + from_partner(give.astype(wire), "layer", level_index).astype(jnp.float32)
        node_index = layers - (layers >> level_index) + (layer_index >> level_index + 1)
        owner_index = sep_owner[node_index]
        pivot_rows = spread(combined.astype(jnp.bfloat16), "grid", owner_index)
        factor = lax.dynamic_index_in_dim(sep_panels, node_index, 0, keepdims=False)
        combined = combined - jnp.dot(factor, pivot_rows, preferred_element_type=jnp.float32)
    return combined


def solution(mesh):
    return jax.shard_map(
        local,
        mesh=mesh,
        in_specs=(
            P("layer", None, "grid", None),
            P("layer", None, "grid", None),
            P("layer", None, "grid", None),
            P("layer", "grid", None),
            P(None, "grid", None),
            P(),
        ),
        out_specs=P("grid", "layer"),
        check_vma=False,
    )
```

```python
import jax
import jax.numpy as jnp
from jax import lax
from jax.experimental import pallas as pl
from jax.experimental.pallas import tpu as pltpu
from jax.sharding import PartitionSpec as P

BLOCK = 128
X = 4
Z = 8
GROUP = BLOCK // X
LEVELS = 4
F32 = jnp.float32
BF16 = jnp.bfloat16


def turned(v, groups):
    shift = groups % X * GROUP
    return pltpu.roll(v, shift, 1) if shift else v


def by_group(pieces):
    group = lax.broadcasted_iota(jnp.int32, pieces[0].shape, 1) // GROUP
    out = pieces[0]
    for g in range(1, X):
        out = jnp.where(group == g, pieces[g], out)
    return out


def by_half(low, high):
    lane = lax.broadcasted_iota(jnp.int32, low.shape, 1)
    return jnp.where(lane < BLOCK // 2, low, high)


def column_block(tile, group):
    return (tile >> 1) + 2 * (tile & 1) + 4 * (group >> 1) + 8 * (group & 1)


def dot(a, b):
    return jnp.dot(a, b, preferred_element_type=F32)


def kernel(
    owner_ref, panel_fill_ref, copy_fill_ref, l_ref, u_ref, sep_ref, out_ref,
    u_row, u_buf, l_buf, mask, acc, other, half, sep_buf,
    give1, take1, state1, pack2, give2, take2, state2, pack3, give3, take3, state3,
    cand0, parts0, pivot0, cand1, parts1, pivot1, slices, final,
    u_sem, mask_sem, l_sem, ring_sem, core_sem, sep_sem, own_sem, y_sem, part_sem, pivot_sem, final_sem,
):
    layer = lax.axis_index("layer")
    grid = lax.axis_index("grid")
    x = grid // Z
    z = grid % Z
    rows = l_ref.shape[2]
    width = l_ref.shape[3]
    panels = l_ref.shape[1]
    depth = u_ref.shape[2]

    def along_x(d):
        return (x + d) % X

    def along_z(d):
        return (z + d) % Z

    def bit(level):
        return layer // 2**level % 2

    def partner(level):
        return layer + 2**level * (1 - 2 * bit(level))

    def remote(src, dst, sems, index, device):
        return pltpu.make_async_remote_copy(
            src_ref=src,
            dst_ref=dst,
            send_sem=sems.at[(0, *index)],
            recv_sem=sems.at[(1, *index)],
            device_id=device,
            device_id_type=pl.DeviceIdType.MESH,
        )

    def to_x(d):
        return {"grid": along_x(d) * Z + z}

    def to_z(d):
        return {"grid": x * Z + along_z(d)}

    barrier = pltpu.get_barrier_semaphore()
    peers = [to_x(d) for d in range(1, X)] + [to_z(d) for d in range(1, Z)]
    peers += [{"layer": partner(level)} for level in range(LEVELS)]
    for peer in peers:
        pl.semaphore_signal(barrier, inc=1, device_id=peer, device_id_type=pl.DeviceIdType.MESH)

    own_sep = []
    for level in range(LEVELS):
        node = 2**LEVELS - (2**LEVELS >> level) + layer // 2 ** (level + 1)
        own_sep.append(pltpu.make_async_copy(sep_ref.at[node], sep_buf.at[level, x], own_sem.at[level]))
        own_sep[level].start()

    turns = {}
    for tile in range(X):
        for group in range(X):
            block = column_block(tile, group)
            piece = u_ref[0, :, :, block * BLOCK : (block + 1) * BLOCK].astype(F32).reshape(panels * depth, BLOCK)
            turns[tile, group] = [turned(piece, n) for n in range(X)]
        for quarter in range(X):
            mixed = by_group([turns[tile, group][(group - quarter) % X] for group in range(X)])
            u_row[quarter, :, :, tile * BLOCK : (tile + 1) * BLOCK] = mixed.astype(BF16).reshape(panels, depth, BLOCK)
    u_buf[:, x, z] = u_row[x]

    pl.semaphore_wait(barrier, len(peers))

    u_copies = []
    for d in range(1, X):
        u_copies.append(remote(u_row.at[along_x(d)], u_buf.at[:, x, z], u_sem, (d - 1,), to_x(d)))
        u_copies[-1].start()

    for k in range(panels):
        for r in range(rows // BLOCK):
            for c in range(width // BLOCK):
                fill = panel_fill_ref[0, k, r, c].astype(F32)
                piece = l_ref[0, k, r * BLOCK : (r + 1) * BLOCK, c * BLOCK : (c + 1) * BLOCK].astype(F32) * fill
                l_buf[x, r * BLOCK : (r + 1) * BLOCK, k * width + c * BLOCK : k * width + (c + 1) * BLOCK] = (
                    piece.astype(BF16)
                )

    def l_copy(index, source, part, d):
        where = l_buf.at[along_x(source), pl.ds(part * BLOCK, BLOCK)]
        return remote(where, where, l_sem, (index,), to_x(d))

    l_copies = [l_copy(0, 0, 0, 1), l_copy(1, 0, 1, -1), l_copy(2, 0, 1, 1), l_copy(3, 0, 0, -1)]
    for copy in l_copies:
        copy.start()

    shape = (8, BLOCK)
    sublane = lax.broadcasted_iota(jnp.int32, shape, 0)
    for tile in range(X):
        picked = []
        for group in range(X):
            value = jnp.zeros(shape, F32)
            for r in range(rows // BLOCK):
                fill = copy_fill_ref[0, r, column_block(tile, group)].astype(F32)
                value = jnp.where(sublane == r, -fill, value)
            picked.append(value)
        mask[x, :, tile * BLOCK : (tile + 1) * BLOCK] = by_group(picked)
    mask_copies = []
    for d in range(1, X):
        mask_copies.append(remote(mask.at[x], mask.at[x], mask_sem, (d - 1,), to_x(d)))
        mask_copies[-1].start()

    for copy in u_copies:
        copy.wait_recv()

    def ring_copy(step, way):
        block = along_z(-way * (step - 1))
        if step < Z // 2:
            where = u_buf.at[:, :, block]
        else:
            where = u_buf.at[0 if way > 0 else 1, :, block]
        return remote(where, where, ring_sem, (2 * (step - 1) + (way < 0),), to_z(way))

    ring = {}
    for step in range(1, Z // 2 + 1):
        for way in (1, -1):
            if step > 1:
                ring[step - 1, way].wait_recv()
            ring[step, way] = ring_copy(step, way)
            ring[step, way].start()
        if step == 2:
            for index, (source, part, way) in enumerate(((-1, 0, 1), (1, 1, -1))):
                l_copies[index].wait_recv()
                l_copies.append(l_copy(4 + index, source, part, way))
                l_copies[-1].start()

    sep_copies = []
    for level in range(LEVELS):
        own_sep[level].wait()
        where = sep_buf.at[level, x]
        sep_copies.append([remote(where, where, sep_sem, (level, d - 1), to_x(d)) for d in range(1, X)])
        for copy in sep_copies[level]:
            copy.start()

    for copy in mask_copies:
        copy.wait_recv()
    for way in (1, -1):
        ring[Z // 2, way].wait_recv()

    def weight(level, row_block):
        node = 2**LEVELS - (2**LEVELS >> level) + layer // 2 ** (level + 1)
        return jnp.where(owner_ref[node] == row_block * Z + z, 1.0, 0.0).astype(F32)

    core_copies = []
    order = [along_x(d) for d in (0, -1, 1, 2)]
    waits = [[], [2], [3], [4, 5]]
    for index, row_block in enumerate(order):
        for which in waits[index]:
            l_copies[which].wait_recv()
        u_all = u_buf[...].reshape(panels * width, X * BLOCK)
        for r in range(rows // BLOCK):
            part = dot(l_buf[row_block, r * BLOCK : (r + 1) * BLOCK], u_all) * mask[row_block, r : r + 1]
            for h in range(2):
                acc[h, row_block, r * BLOCK : (r + 1) * BLOCK] = part[:, h * 2 * BLOCK : (h + 1) * 2 * BLOCK]
        core_copies.append(
            remote(acc.at[1 - bit(0), row_block], other.at[row_block], core_sem, (index,), {"layer": partner(0)})
        )
        core_copies[-1].start()

    def spread(level, cand, parts, pivot):
        def part_copy(d):
            return remote(cand.at[:, along_z(d)], parts.at[d], part_sem, (level, d), to_z(d))

        def pivot_copy(d):
            where = pivot.at[:, z]
            return remote(where, where, pivot_sem, (level, d), to_z(d))

        def each(act):
            def body(d, carry):
                act(d)
                return carry

            lax.fori_loop(1, Z, body, 0)

        each(lambda d: part_copy(d).start())
        total = cand[:, z].astype(F32)

        def add(d, total):
            part_copy(d).wait_recv()
            return total + parts[d].astype(F32)

        total = lax.fori_loop(1, Z, add, total)
        pivot[:, z] = total.astype(BF16)
        each(lambda d: pivot_copy(d).start())
        each(lambda d: pivot_copy(d).wait_recv())
        each(lambda d: part_copy(d).wait_send())
        each(lambda d: pivot_copy(d).wait_send())

    picked = jnp.zeros((rows, 2 * BLOCK), F32)
    for index, row_block in enumerate(order):
        core_copies[index].wait_recv()
        value = acc[bit(0), row_block] + other[row_block]
        for h in range(2):
            half[h, row_block] = value[:, h * BLOCK : (h + 1) * BLOCK]
        picked = picked + weight(0, row_block) * value
    for h in range(2):
        cand0[h] = picked[:, h * BLOCK : (h + 1) * BLOCK].astype(BF16).reshape(Z, rows // Z, BLOCK)
    spread(0, cand0, parts0, pivot0)

    for copy in sep_copies[0]:
        copy.wait_recv()
    y_copies = []
    giving = 1 - bit(1)
    for row_block in range(X):
        update = dot(sep_buf[0, row_block], pivot0[giving].reshape(rows, BLOCK))
        give1[row_block] = (half[giving, row_block] - update).astype(BF16)
        y_copies.append(
            remote(give1.at[row_block], take1.at[row_block], y_sem, (row_block,), {"layer": partner(1)})
        )
        y_copies[-1].start()
    picked = jnp.zeros((rows, BLOCK), F32)
    for row_block in range(X):
        update = dot(sep_buf[0, row_block], pivot0[bit(1)].reshape(rows, BLOCK))
        value = half[bit(1), row_block] - update
        y_copies[row_block].wait_recv()
        value = value + take1[row_block].astype(F32)
        state1[row_block] = value
        picked = picked + weight(1, row_block) * value
    cand1[0, 0] = picked.astype(BF16).reshape(Z, rows // Z, BLOCK)
    spread(1, cand1.at[0], parts1.at[0], pivot1.at[0])

    for copy in sep_copies[1]:
        copy.wait_recv()
    for pair in range(2):
        low, high = [
            state1[row_block] - dot(sep_buf[1, row_block], pivot1[0, 0].reshape(rows, BLOCK))
            for row_block in (pair, pair + 2)
        ]
        pack2[0, pair] = by_half(low, turned(high, 2))
        pack2[1, pair] = by_half(turned(low, 2), high)
    give2[...] = pack2[1 - bit(2)].astype(BF16)
    y_copies.append(remote(give2, take2, y_sem, (X,), {"layer": partner(2)}))
    y_copies[-1].start()
    y_copies[-1].wait_recv()
    value = pack2[bit(2)] + take2[...].astype(F32)
    state2[...] = value
    picked = by_half(*[weight(2, 2 * h) * value[0] + weight(2, 2 * h + 1) * value[1] for h in range(2)])
    picked = picked + turned(picked, 2)
    cand1[1, 0] = picked.astype(BF16).reshape(Z, rows // Z, BLOCK)
    spread(2, cand1.at[1], parts1.at[1], pivot1.at[1])

    for copy in sep_copies[2]:
        copy.wait_recv()
    updates = [dot(sep_buf[2, row_block], pivot1[1, 0].reshape(rows, BLOCK)) for row_block in range(X)]
    even, odd = [state2[pair] - by_half(updates[pair], updates[pair + 2]) for pair in range(2)]
    moved_even, moved_odd = turned(even, -1), turned(odd, 1)
    pack3[0] = by_group([even, moved_odd, even, moved_odd])
    pack3[1] = by_group([moved_even, odd, moved_even, odd])
    give3[...] = pack3[1 - bit(3)].astype(BF16)
    y_copies.append(remote(give3, take3, y_sem, (X + 1,), {"layer": partner(3)}))
    y_copies[-1].start()
    y_copies[-1].wait_recv()
    value = pack3[bit(3)] + take3[...].astype(F32)
    state3[...] = value
    picked = by_group([weight(3, g) * value for g in range(X)])
    picked = picked + turned(picked, 1)
    picked = picked + turned(picked, 2)
    cand1[2, 0] = picked.astype(BF16).reshape(Z, rows // Z, BLOCK)
    spread(3, cand1.at[2], parts1.at[2], pivot1.at[2])
    for copy in sep_copies[3]:
        copy.wait_recv()
    updates = [dot(sep_buf[3, row_block], pivot1[2, 0].reshape(rows, BLOCK)) for row_block in range(X)]
    value = state3[...] - by_group(updates)

    quarter = rows // X
    for row_block in range(X):
        slices[row_block] = by_group(
            [turned(value[k * quarter : (k + 1) * quarter], k - row_block) for k in range(X)]
        )
    final_copies = []
    for d in range(1, X):
        final_copies.append(remote(slices.at[along_x(d)], final.at[x], final_sem, (d - 1,), to_x(d)))
        final_copies[-1].start()
    final[x] = slices[x]
    for copy in final_copies:
        copy.wait_recv()
    for k in range(X):
        out_ref[k * quarter : (k + 1) * quarter, :] = by_group([turned(final[q], q - k) for q in range(X)])

    started = u_copies + mask_copies + l_copies + list(ring.values()) + core_copies + y_copies + final_copies
    for copy in started + [copy for level in sep_copies for copy in level]:
        copy.wait_send()


def local(l_panels, u_panels, panel_fill, copy_fill, sep_panels, sep_owner):
    _, panels, rows, width = l_panels.shape
    depth, columns = u_panels.shape[2:]
    quarter = columns // X
    remote_sems = [
        (X - 1,), (X - 1,), (6,), (Z,), (X,), (LEVELS, X - 1), None, (X + 2,), (LEVELS, Z), (LEVELS, Z), (X - 1,),
    ]
    smem = pl.BlockSpec(memory_space=pltpu.SMEM)
    vmem = pl.BlockSpec(memory_space=pltpu.VMEM)
    return pl.pallas_call(
        kernel,
        out_shape=jax.ShapeDtypeStruct((rows, BLOCK), F32),
        in_specs=[smem, smem, smem, vmem, vmem, pl.BlockSpec(memory_space=pl.ANY)],
        out_specs=vmem,
        scratch_shapes=[
            pltpu.VMEM((X, panels, depth, quarter), BF16),
            pltpu.VMEM((panels, X, Z, depth, quarter), BF16),
            pltpu.VMEM((X, rows, panels * width), BF16),
            pltpu.VMEM((X, 8, quarter), F32),
            pltpu.VMEM((2, X, rows, 2 * BLOCK), F32),
            pltpu.VMEM((X, rows, 2 * BLOCK), F32),
            pltpu.VMEM((2, X, rows, BLOCK), F32),
            pltpu.VMEM((LEVELS, X, rows, sep_panels.shape[2]), BF16),
            pltpu.VMEM((X, rows, BLOCK), BF16),
            pltpu.VMEM((X, rows, BLOCK), BF16),
            pltpu.VMEM((X, rows, BLOCK), F32),
            pltpu.VMEM((2, 2, rows, BLOCK), F32),
            pltpu.VMEM((2, rows, BLOCK), BF16),
            pltpu.VMEM((2, rows, BLOCK), BF16),
            pltpu.VMEM((2, rows, BLOCK), F32),
            pltpu.VMEM((2, rows, BLOCK), F32),
            pltpu.VMEM((rows, BLOCK), BF16),
            pltpu.VMEM((rows, BLOCK), BF16),
            pltpu.VMEM((rows, BLOCK), F32),
            pltpu.VMEM((2, Z, rows // Z, BLOCK), BF16),
            pltpu.VMEM((Z, 2, rows // Z, BLOCK), BF16),
            pltpu.VMEM((2, Z, rows // Z, BLOCK), BF16),
            pltpu.VMEM((3, 1, Z, rows // Z, BLOCK), BF16),
            pltpu.VMEM((3, Z, 1, rows // Z, BLOCK), BF16),
            pltpu.VMEM((3, 1, Z, rows // Z, BLOCK), BF16),
            pltpu.VMEM((X, rows // X, BLOCK), F32),
            pltpu.VMEM((X, rows // X, BLOCK), F32),
            *[pltpu.SemaphoreType.DMA((LEVELS,) if s is None else (2, *s)) for s in remote_sems],
        ],
        compiler_params=pltpu.CompilerParams(
            collective_id=0, has_side_effects=True, vmem_limit_bytes=40 * 2**20
        ),
        cost_estimate=pl.CostEstimate(flops=2**31, bytes_accessed=2**22, transcendentals=0),
    )(sep_owner, panel_fill, copy_fill, l_panels, u_panels, sep_panels)


def solution(mesh):
    return jax.shard_map(
        local,
        mesh=mesh,
        in_specs=(
            P("layer", None, "grid", None),
            P("layer", None, "grid", None),
            P("layer", None, "grid", None),
            P("layer", "grid", None),
            P(None, "grid", None),
            P(),
        ),
        out_specs=P("grid", "layer"),
        check_vma=False,
    )
```

```python
import jax
import jax.numpy as jnp
from jax import lax
from jax.experimental import pallas as pl
from jax.experimental.pallas import tpu as pltpu
from jax.sharding import PartitionSpec as P

BLOCK = 128
X = 4
Z = 8
GROUP = BLOCK // X
LEVELS = 4
F32 = jnp.float32
BF16 = jnp.bfloat16


def turned(v, groups):
    shift = groups % X * GROUP
    return pltpu.roll(v, shift, 1) if shift else v


def by_group(pieces):
    group = lax.broadcasted_iota(jnp.int32, pieces[0].shape, 1) // GROUP
    out = pieces[0]
    for g in range(1, X):
        out = jnp.where(group == g, pieces[g], out)
    return out


def by_half(low, high):
    lane = lax.broadcasted_iota(jnp.int32, low.shape, 1)
    return jnp.where(lane < BLOCK // 2, low, high)


def column_block(tile, group):
    return (tile >> 1) + 2 * (tile & 1) + 4 * (group >> 1) + 8 * (group & 1)


def dot(a, b):
    return jnp.dot(a, b, preferred_element_type=F32)


def kernel(
    owner_any, panel_fill_any, copy_fill_any, l_any, u_any, sep_ref, out_ref,
    owner_ref, panel_fill_ref, copy_fill_ref, l_ref, u_ref,
    u_row, u_buf, l_buf, mask, acc, other, half, sep_buf,
    give1, take1, state1, pack2, give2, take2, state2, pack3, give3, take3, state3,
    cand0, parts0, chunk0, pivot0, cand1, parts1, chunk1, pivot1, cand2, parts2, chunk2, pivot2, cand3, parts3,
    slices, final,
    u_sem, mask_sem, l_sem, ring_sem, core_sem, sep_sem, pass_sem, own_sem, y_sem, part_sem, pivot_sem, final_sem,
):
    layer = lax.axis_index("layer")
    grid = lax.axis_index("grid")
    x = grid // Z
    z = grid % Z
    rows = l_ref.shape[2]
    width = l_ref.shape[3]
    panels = l_ref.shape[1]
    depth = u_ref.shape[2]

    def along_x(d):
        return (x + d) % X

    def along_z(d):
        return (z + d) % Z

    def bit(level):
        return layer // 2**level % 2

    def partner(level):
        return layer + 2**level * (1 - 2 * bit(level))

    def remote(src, dst, sems, index, device):
        return pltpu.make_async_remote_copy(
            src_ref=src,
            dst_ref=dst,
            send_sem=sems.at[(0, *index)],
            recv_sem=sems.at[(1, *index)],
            device_id=device,
            device_id_type=pl.DeviceIdType.MESH,
        )

    def to_x(d):
        return {"grid": along_x(d) * Z + z}

    def to_z(d):
        return {"grid": x * Z + along_z(d)}

    def across(level, d):
        return {"layer": partner(level), "grid": x * Z + along_z(d)}

    def node(level, sibling):
        group = layer // 2 ** (level + 1)
        if sibling:
            group = group + 1 - 2 * (group % 2)
        return 2**LEVELS - (2**LEVELS >> level) + group

    barrier = pltpu.get_barrier_semaphore()
    peers = [to_x(d) for d in range(1, X)] + [to_z(d) for d in range(1, Z)]
    peers += [across(0, 0)] + [across(level, d) for level in range(1, LEVELS) for d in range(Z)]
    for peer in peers:
        pl.semaphore_signal(barrier, inc=1, device_id=peer, device_id_type=pl.DeviceIdType.MESH)

    pairs = ((u_any, u_ref), (panel_fill_any, panel_fill_ref), (l_any, l_ref), (copy_fill_any, copy_fill_ref), (owner_any, owner_ref))
    loads = [pltpu.make_async_copy(src, dst, own_sem.at[i]) for i, (src, dst) in enumerate(pairs)]
    for load in loads:
        load.start()
    load_u, load_panel_fill, load_l, load_copy_fill, load_owner = loads
    items = [(level, sibling) for level in range(LEVELS) for sibling in range(2)][:-1]
    own_sep = []
    for i, (level, sibling) in enumerate(items):
        own_sep.append(
            pltpu.make_async_copy(sep_ref.at[node(level, sibling)], sep_buf.at[i, x], own_sem.at[len(loads) + i])
        )
        own_sep[i].start()

    load_u.wait()
    turns = {}
    for tile in range(X):
        for group in range(X):
            block = column_block(tile, group)
            piece = u_ref[0, :, :, block * BLOCK : (block + 1) * BLOCK].astype(F32).reshape(panels * depth, BLOCK)
            turns[tile, group] = [turned(piece, n) for n in range(X)]
        for quarter in range(X):
            mixed = by_group([turns[tile, group][(group - quarter) % X] for group in range(X)])
            u_row[quarter, :, :, tile * BLOCK : (tile + 1) * BLOCK] = mixed.astype(BF16).reshape(panels, depth, BLOCK)
    u_buf[:, x, z] = u_row[x]

    load_panel_fill.wait()
    load_l.wait()
    for r in range(rows // BLOCK):
        for k in range(panels):
            for c in range(width // BLOCK):
                fill = panel_fill_ref[0, k, r, c].astype(F32)
                piece = l_ref[0, k, r * BLOCK : (r + 1) * BLOCK, c * BLOCK : (c + 1) * BLOCK].astype(F32) * fill
                l_buf[x, r * BLOCK : (r + 1) * BLOCK, k * width + c * BLOCK : k * width + (c + 1) * BLOCK] = (
                    piece.astype(BF16)
                )

    load_copy_fill.wait()
    load_owner.wait()
    shape = (8, BLOCK)
    sublane = lax.broadcasted_iota(jnp.int32, shape, 0)
    for tile in range(X):
        picked = []
        for group in range(X):
            value = jnp.zeros(shape, F32)
            for r in range(rows // BLOCK):
                fill = copy_fill_ref[0, r, column_block(tile, group)].astype(F32)
                value = jnp.where(sublane == r, -fill, value)
            picked.append(value)
        mask[x, :, tile * BLOCK : (tile + 1) * BLOCK] = by_group(picked)

    pl.semaphore_wait(barrier, len(peers))

    u_copies = []
    for d in range(1, X):
        u_copies.append(remote(u_row.at[along_x(d)], u_buf.at[:, x, z], u_sem, (d - 1,), to_x(d)))
        u_copies[-1].start()

    def ring_copy(step, index, way):
        block = along_z(-way * (step - 1))
        source = along_x((0, -1, 1, 2)[index])
        if step < Z // 2:
            where = u_buf.at[:, source, block]
        else:
            where = u_buf.at[0 if way > 0 else 1, source, block]
        return remote(where, where, ring_sem, (Z * index + 2 * (step - 1) + (way < 0),), to_z(way))

    ring = {}

    def ring_step(step, index):
        if step == 1 and index:
            u_copies[(None, 0, 2, 1)[index]].wait_recv()
        for way in (1, -1):
            if step > 1:
                ring[step - 1, index, way].wait_recv()
            if step <= Z // 2:
                ring[step, index, way] = ring_copy(step, index, way)
                ring[step, index, way].start()

    ring_step(1, 0)

    def l_copy(index, source, part, d):
        where = l_buf.at[along_x(source), pl.ds(part * BLOCK, BLOCK)]
        return remote(where, where, l_sem, (index,), to_x(d))

    l_copies = [l_copy(0, 0, 0, 1), l_copy(1, 0, 1, -1), l_copy(2, 0, 1, 1), l_copy(3, 0, 0, -1)]
    for copy in l_copies:
        copy.start()
    mask_copies = []
    for d in range(1, X):
        mask_copies.append(remote(mask.at[x], mask.at[x], mask_sem, (d - 1,), to_x(d)))
        mask_copies[-1].start()

    for index in range(1, X):
        ring_step(1, index)
    for step in range(2, Z // 2 + 2):
        for index in range(X):
            ring_step(step, index)
        if step == 2:
            for index, (source, part, way) in enumerate(((-1, 0, 1), (1, 1, -1))):
                l_copies[index].wait_recv()
                l_copies.append(l_copy(4 + index, source, part, way))
                l_copies[-1].start()

    way = 1 - 2 * bit(0)
    beside, opposite = along_x(-way), along_x(2)

    sep_copies = [[] for _ in items]

    def sep_copy(i, where, sems, index, device):
        sep_copies[i].append(remote(where, where, sems, (i, index), device))
        sep_copies[i][-1].start()

    def sep_start(i):
        own_sep[i].wait()
        sep_copy(i, sep_buf.at[i, x], sep_sem, 0, to_x(way))

    def sep_forward(i):
        sep_copies[i][0].wait_recv()
        sep_copy(i, sep_buf.at[i, beside, pl.ds(bit(0) * BLOCK, BLOCK)], sep_sem, 1, to_x(way))
        sep_copy(i, sep_buf.at[i, beside], pass_sem, 0, across(0, 0))

    def sep_finish(i):
        sep_copies[i][1].wait_recv()
        sep_copy(i, sep_buf.at[i, opposite, pl.ds(bit(0) * BLOCK, BLOCK)], pass_sem, 1, across(0, 0))

    def sep_wait(i):
        sep_copies[i][2].wait_recv()
        sep_copies[i][3].wait_recv()

    for copy in mask_copies:
        copy.wait_recv()

    def weight(level, row_block):
        return jnp.where(owner_ref[node(level, 0)] == row_block * Z + z, 1.0, 0.0).astype(F32)

    core_copies = []
    y_copies = []
    order = [along_x(d) for d in (0, -1, 1, 2)]
    waits = [[], [2], [3], [4, 5]]
    giving = 1 - bit(1)
    total0 = [jnp.zeros((rows, BLOCK), F32) for _ in range(2)]
    for index in range(X + 1):
        if index < X:
            row_block = order[index]
            for which in waits[index]:
                l_copies[which].wait_recv()
            if index == X - 1:
                sep_start(0)
                sep_start(1)
            u_all = u_buf[...].reshape(panels * width, X * BLOCK)
            for r in range(rows // BLOCK):
                part = dot(l_buf[row_block, r * BLOCK : (r + 1) * BLOCK], u_all) * mask[row_block, r : r + 1]
                for h in range(2):
                    acc[h, row_block, r * BLOCK : (r + 1) * BLOCK] = part[:, h * 2 * BLOCK : (h + 1) * 2 * BLOCK]
            core_copies.append(
                remote(acc.at[1 - bit(0), row_block], other.at[row_block], core_sem, (index,), across(0, 0))
            )
            core_copies[-1].start()
        if index:
            row_block = order[index - 1]
            core_copies[index - 1].wait_recv()
            value = acc[bit(0), row_block] + other[row_block]
            for h in range(2):
                half[h, row_block] = value[:, h * BLOCK : (h + 1) * BLOCK]
                total0[h] = total0[h] + weight(0, row_block) * value[:, h * BLOCK : (h + 1) * BLOCK]
            give1[row_block] = half[giving, row_block].astype(BF16)
            y_copies.append(remote(give1.at[row_block], take1.at[row_block], y_sem, (index - 1,), across(1, 0)))
            y_copies[-1].start()

    late = []

    def each(low, act):
        def body(d, carry):
            act(d)
            return carry

        lax.fori_loop(low, Z, body, 0)

    def part_copies(level, cand, parts):
        return lambda d: remote(cand.at[along_z(d)], parts.at[d], part_sem, (level, d), to_z(d))

    def add_parts(own, parts, copies):
        def add(d, total):
            copies(d).wait_recv()
            return total + parts[d].astype(F32)

        total = lax.fori_loop(1, Z, add, own.astype(F32))
        late.append((1, copies))
        return total

    def pivot_start(level, mine, theirs, pivot):
        def here(d):
            return remote(mine, pivot.at[0, z], pivot_sem, (level, d), to_z(d))

        def there(d):
            return remote(theirs, pivot.at[1, z], pivot_sem, (level, Z + d), across(level + 1, d))

        each(1, lambda d: here(d).start())
        each(0, lambda d: there(d).start())
        pivot[0, z] = mine[...]
        return here, there

    def pivot_wait(copies):
        here, there = copies
        each(1, lambda d: here(d).wait_recv())
        each(0, lambda d: there(d).wait_recv())
        late.extend([(1, here), (0, there)])

    def update(level, row_block, pivots):
        return sum(dot(sep_buf[2 * level + i, row_block], pivot) for i, pivot in enumerate(pivots))

    for h in range(2):
        cand0[:, h] = total0[h].astype(BF16).reshape(Z, rows // Z, BLOCK)
    copies = part_copies(0, cand0, parts0)
    each(1, lambda d: copies(d).start())
    for i in (0, 1):
        sep_forward(i)
    for i in range(2, len(items)):
        sep_start(i)
    chunk0[...] = add_parts(cand0[z], parts0, copies).astype(BF16)
    copies = pivot_start(0, chunk0.at[bit(1)], chunk0.at[giving], pivot0)
    for i in (0, 1):
        sep_finish(i)
    for i in (0, 1):
        sep_wait(i)
    pivot_wait(copies)

    picked = jnp.zeros((rows, BLOCK), F32)
    pivots = [pivot0[i].reshape(rows, BLOCK) for i in range(2)]
    for copy in y_copies:
        copy.wait_recv()
    for row_block in range(X):
        value = half[bit(1), row_block] - update(0, row_block, pivots)
        value = value + take1[row_block].astype(F32)
        state1[row_block] = value
        picked = picked + weight(1, row_block) * value
    cand1[...] = picked.astype(BF16).reshape(Z, rows // Z, BLOCK)
    copies = part_copies(1, cand1, parts1)
    each(1, lambda d: copies(d).start())

    def pack_two(blocks):
        for pair in range(2):
            low, high = blocks[pair], blocks[pair + 2]
            pack2[0, pair] = by_half(low, turned(high, 2))
            pack2[1, pair] = by_half(turned(low, 2), high)

    pack_two([state1[row_block] for row_block in range(X)])
    give2[...] = pack2[1 - bit(2)].astype(BF16)
    y_copies.append(remote(give2, take2, y_sem, (X,), across(2, 0)))
    y_copies[-1].start()
    for i in (2, 3):
        sep_forward(i)
    chunk1[...] = add_parts(cand1[z], parts1, copies).astype(BF16)
    copies = pivot_start(1, chunk1, chunk1, pivot1)
    for i in (2, 3):
        sep_finish(i)
    for i in (2, 3):
        sep_wait(i)
    pivot_wait(copies)

    pivots = [pivot1[i].reshape(rows, BLOCK) for i in range(2)]
    pack_two([state1[row_block] - update(1, row_block, pivots) for row_block in range(X)])
    y_copies[-1].wait_recv()
    value = pack2[bit(2)] + take2[...].astype(F32)
    state2[...] = value
    picked = by_half(*[weight(2, 2 * h) * value[0] + weight(2, 2 * h + 1) * value[1] for h in range(2)])
    picked = picked + turned(picked, 2)
    picked = by_half(picked[: rows // 2], picked[rows // 2 :])
    cand2[...] = picked.astype(BF16).reshape(Z, rows // Z // 2, BLOCK)
    copies = part_copies(2, cand2, parts2)
    each(1, lambda d: copies(d).start())

    def pack_four(even, odd):
        moved_even, moved_odd = turned(even, -1), turned(odd, 1)
        pack3[0] = by_group([even, moved_odd, even, moved_odd])
        pack3[1] = by_group([moved_even, odd, moved_even, odd])

    pack_four(state2[0], state2[1])
    give3[...] = pack3[1 - bit(3)].astype(BF16)
    y_copies.append(remote(give3, take3, y_sem, (X + 1,), across(3, 0)))
    y_copies[-1].start()
    for i in (4, 5, 6):
        sep_forward(i)
    chunk2[...] = add_parts(cand2[z], parts2, copies).astype(BF16)
    copies = pivot_start(2, chunk2, chunk2, pivot2)
    for i in (4, 5, 6):
        sep_finish(i)
    for i in (4, 5, 6):
        sep_wait(i)
    pivot_wait(copies)

    pivots = []
    for i in range(2):
        packed = pivot2[i].astype(F32).reshape(rows // 2, BLOCK)
        moved = turned(packed, 2)
        pivots.append(jnp.concatenate([by_half(packed, moved), by_half(moved, packed)], axis=0).astype(BF16))
    updates = [update(2, row_block, pivots) for row_block in range(X)]
    pack_four(*[state2[pair] - by_half(updates[pair], updates[pair + 2]) for pair in range(2)])
    y_copies[-1].wait_recv()
    value = pack3[bit(3)] + take3[...].astype(F32)
    state3[...] = value
    picked = by_group([weight(3, g) * value for g in range(X)])
    picked = picked + turned(picked, 1)
    picked = picked + turned(picked, 2)
    quarter = rows // X
    cand3[...] = by_group([picked[k * quarter : (k + 1) * quarter] for k in range(X)]).astype(BF16)

    def whole_copies(d):
        return remote(cand3, parts3.at[d], part_sem, (3, d), to_z(d))

    each(1, lambda d: whole_copies(d).start())
    packed = add_parts(cand3[...], parts3, whole_copies)
    pivot = []
    for k in range(X):
        nothing = jnp.zeros_like(packed)
        one = by_group([packed if g == k else nothing for g in range(X)])
        one = one + turned(one, 1)
        pivot.append(one + turned(one, 2))
    pivot = jnp.concatenate(pivot, axis=0).astype(BF16)
    value = state3[...] - by_group([update(3, row_block, [pivot]) for row_block in range(X)])

    for row_block in range(X):
        slices[row_block] = by_group(
            [turned(value[k * quarter : (k + 1) * quarter], k - row_block) for k in range(X)]
        )
    final_copies = []
    for d in range(1, X):
        final_copies.append(remote(slices.at[along_x(d)], final.at[x], final_sem, (d - 1,), to_x(d)))
        final_copies[-1].start()
    final[x] = slices[x]
    for copy in final_copies:
        copy.wait_recv()
    for k in range(X):
        out_ref[k * quarter : (k + 1) * quarter, :] = by_group([turned(final[q], q - k) for q in range(X)])

    started = u_copies + mask_copies + l_copies + list(ring.values()) + core_copies + y_copies + final_copies
    for copy in started + [copy for item in sep_copies for copy in item]:
        copy.wait_send()
    for low, copies in late:
        each(low, lambda d, copies=copies: copies(d).wait_send())


def local(l_panels, u_panels, panel_fill, copy_fill, sep_panels, sep_owner):
    _, panels, rows, width = l_panels.shape
    depth, columns = u_panels.shape[2:]
    quarter = columns // X
    items = 2 * LEVELS - 1
    remote_sems = [
        (X - 1,), (X - 1,), (6,), (X * Z,), (X,), (items, 2), (items, 2), None, (X + 2,), (LEVELS, Z),
        (LEVELS - 1, 2 * Z), (X - 1,),
    ]
    chunk = rows // Z
    kept = pl.BlockSpec(memory_space=pl.ANY)
    return pl.pallas_call(
        kernel,
        out_shape=jax.ShapeDtypeStruct((rows, BLOCK), F32),
        in_specs=[kept] * 6,
        out_specs=pl.BlockSpec(memory_space=pltpu.VMEM),
        scratch_shapes=[
            pltpu.SMEM(sep_owner.shape, jnp.int32),
            pltpu.SMEM(panel_fill.shape, jnp.int32),
            pltpu.SMEM(copy_fill.shape, jnp.int32),
            pltpu.VMEM(l_panels.shape, BF16),
            pltpu.VMEM(u_panels.shape, BF16),
            pltpu.VMEM((X, panels, depth, quarter), BF16),
            pltpu.VMEM((panels, X, Z, depth, quarter), BF16),
            pltpu.VMEM((X, rows, panels * width), BF16),
            pltpu.VMEM((X, 8, quarter), F32),
            pltpu.VMEM((2, X, rows, 2 * BLOCK), F32),
            pltpu.VMEM((X, rows, 2 * BLOCK), F32),
            pltpu.VMEM((2, X, rows, BLOCK), F32),
            pltpu.VMEM((items, X, rows, sep_panels.shape[2]), BF16),
            pltpu.VMEM((X, rows, BLOCK), BF16),
            pltpu.VMEM((X, rows, BLOCK), BF16),
            pltpu.VMEM((X, rows, BLOCK), F32),
            pltpu.VMEM((2, 2, rows, BLOCK), F32),
            pltpu.VMEM((2, rows, BLOCK), BF16),
            pltpu.VMEM((2, rows, BLOCK), BF16),
            pltpu.VMEM((2, rows, BLOCK), F32),
            pltpu.VMEM((2, rows, BLOCK), F32),
            pltpu.VMEM((rows, BLOCK), BF16),
            pltpu.VMEM((rows, BLOCK), BF16),
            pltpu.VMEM((rows, BLOCK), F32),
            pltpu.VMEM((Z, 2, chunk, BLOCK), BF16),
            pltpu.VMEM((Z, 2, chunk, BLOCK), BF16),
            pltpu.VMEM((2, chunk, BLOCK), BF16),
            pltpu.VMEM((2, Z, chunk, BLOCK), BF16),
            pltpu.VMEM((Z, chunk, BLOCK), BF16),
            pltpu.VMEM((Z, chunk, BLOCK), BF16),
            pltpu.VMEM((chunk, BLOCK), BF16),
            pltpu.VMEM((2, Z, chunk, BLOCK), BF16),
            pltpu.VMEM((Z, chunk // 2, BLOCK), BF16),
            pltpu.VMEM((Z, chunk // 2, BLOCK), BF16),
            pltpu.VMEM((chunk // 2, BLOCK), BF16),
            pltpu.VMEM((2, Z, chunk // 2, BLOCK), BF16),
            pltpu.VMEM((rows // X, BLOCK), BF16),
            pltpu.VMEM((Z, rows // X, BLOCK), BF16),
            pltpu.VMEM((X, rows // X, BLOCK), F32),
            pltpu.VMEM((X, rows // X, BLOCK), F32),
            *[pltpu.SemaphoreType.DMA((items + 5,) if s is None else (2, *s)) for s in remote_sems],
        ],
        compiler_params=pltpu.CompilerParams(
            collective_id=0, has_side_effects=True, vmem_limit_bytes=60 * 2**20
        ),
        cost_estimate=pl.CostEstimate(flops=2**31, bytes_accessed=2**22, transcendentals=0),
    )(sep_owner, panel_fill, copy_fill, l_panels, u_panels, sep_panels)


def solution(mesh):
    return jax.shard_map(
        local,
        mesh=mesh,
        in_specs=(
            P("layer", None, "grid", None),
            P("layer", None, "grid", None),
            P("layer", None, "grid", None),
            P("layer", "grid", None),
            P(None, "grid", None),
            P(),
        ),
        out_specs=P("grid", "layer"),
        check_vma=False,
    )
```

```python
import jax
import jax.numpy as jnp
from jax import lax
from jax.experimental import pallas as pl
from jax.experimental.pallas import tpu as pltpu
from jax.sharding import PartitionSpec as P

BLOCK = 128
X = 4
Z = 8
GROUP = BLOCK // X
LEVELS = 4
F32 = jnp.float32
BF16 = jnp.bfloat16


def turned(v, groups):
    shift = groups % X * GROUP
    return pltpu.roll(v, shift, 1) if shift else v


def by_group(pieces):
    group = lax.broadcasted_iota(jnp.int32, pieces[0].shape, 1) // GROUP
    out = pieces[0]
    for g in range(1, X):
        out = jnp.where(group == g, pieces[g], out)
    return out


def by_half(low, high):
    lane = lax.broadcasted_iota(jnp.int32, low.shape, 1)
    return jnp.where(lane < BLOCK // 2, low, high)


def column_block(tile, group):
    return (tile >> 1) + 2 * (tile & 1) + 4 * (group >> 1) + 8 * (group & 1)


def dot(a, b):
    return jnp.dot(a, b, preferred_element_type=F32)


def kernel(
    owner_any, panel_fill_any, copy_fill_any, l_any, u_any, sep_ref, out_ref,
    owner_ref, panel_fill_ref, copy_fill_ref, l_ref, u_ref,
    u_row, u_buf, l_buf, mask, acc, other, half, sep_buf,
    give1, take1, state1, pack2, give2, take2, state2, pack3, give3, take3, state3,
    cand0, parts0, chunk0, pivot0, cand1, parts1, chunk1, pivot1, cand2, parts2, chunk2, pivot2, cand3, parts3,
    slices, final, corner, corner_parts, corner_chunk, pack_chunk,
    u_sem, mask_sem, l_sem, ring_sem, core_sem, sep_sem, pass_sem, own_sem, y_sem, part_sem, pivot_sem, final_sem,
    corner_sem, corner_pass_sem, ready_sem,
):
    layer = lax.axis_index("layer")
    grid = lax.axis_index("grid")
    x = grid // Z
    z = grid % Z
    rows = l_ref.shape[2]
    width = l_ref.shape[3]
    panels = l_ref.shape[1]
    depth = u_ref.shape[2]

    def along_x(d):
        return (x + d) % X

    def along_z(d):
        return (z + d) % Z

    def bit(level):
        return layer // 2**level % 2

    def partner(level):
        return layer + 2**level * (1 - 2 * bit(level))

    def remote(src, dst, sems, index, device):
        return pltpu.make_async_remote_copy(
            src_ref=src,
            dst_ref=dst,
            send_sem=sems.at[(0, *index)],
            recv_sem=sems.at[(1, *index)],
            device_id=device,
            device_id_type=pl.DeviceIdType.MESH,
        )

    def to_x(d):
        return {"grid": along_x(d) * Z + z}

    def to_z(d):
        return {"grid": x * Z + along_z(d)}

    def across(level, d):
        return {"layer": partner(level), "grid": x * Z + along_z(d)}

    def node(level, sibling):
        group = layer // 2 ** (level + 1)
        if sibling:
            group = group + 1 - 2 * (group % 2)
        return 2**LEVELS - (2**LEVELS >> level) + group

    barrier = pltpu.get_barrier_semaphore()
    peers = [to_x(d) for d in range(1, X)] + [to_z(d) for d in range(1, Z)]
    peers += [across(level, 0) for level in range(LEVELS)]
    for peer in peers:
        pl.semaphore_signal(barrier, inc=1, device_id=peer, device_id_type=pl.DeviceIdType.MESH)

    pairs = ((u_any, u_ref), (panel_fill_any, panel_fill_ref), (l_any, l_ref), (copy_fill_any, copy_fill_ref), (owner_any, owner_ref))
    loads = [pltpu.make_async_copy(src, dst, own_sem.at[i]) for i, (src, dst) in enumerate(pairs)]
    for load in loads:
        load.start()
    load_u, load_panel_fill, load_l, load_copy_fill, load_owner = loads
    items = [(level, sibling) for level in range(LEVELS) for sibling in range(2)][:-1]
    own_sep = []
    for i, (level, sibling) in enumerate(items):
        own_sep.append(
            pltpu.make_async_copy(sep_ref.at[node(level, sibling)], sep_buf.at[i, x], own_sem.at[len(loads) + i])
        )
        own_sep[i].start()

    load_u.wait()
    turns = {}
    for tile in range(X):
        for group in range(X):
            block = column_block(tile, group)
            piece = u_ref[0, :, :, block * BLOCK : (block + 1) * BLOCK].astype(F32).reshape(panels * depth, BLOCK)
            turns[tile, group] = [turned(piece, n) for n in range(X)]
        for quarter in range(X):
            mixed = by_group([turns[tile, group][(group - quarter) % X] for group in range(X)])
            u_row[quarter, :, :, tile * BLOCK : (tile + 1) * BLOCK] = mixed.astype(BF16).reshape(panels, depth, BLOCK)
    u_buf[:, x, z] = u_row[x]

    load_panel_fill.wait()
    load_l.wait()
    for r in range(rows // BLOCK):
        for k in range(panels):
            for c in range(width // BLOCK):
                fill = panel_fill_ref[0, k, r, c].astype(F32)
                piece = l_ref[0, k, r * BLOCK : (r + 1) * BLOCK, c * BLOCK : (c + 1) * BLOCK].astype(F32) * fill
                l_buf[x, r * BLOCK : (r + 1) * BLOCK, k * width + c * BLOCK : k * width + (c + 1) * BLOCK] = (
                    piece.astype(BF16)
                )

    load_copy_fill.wait()
    load_owner.wait()
    shape = (8, BLOCK)
    sublane = lax.broadcasted_iota(jnp.int32, shape, 0)
    for tile in range(X):
        picked = []
        for group in range(X):
            value = jnp.zeros(shape, F32)
            for r in range(rows // BLOCK):
                fill = copy_fill_ref[0, r, column_block(tile, group)].astype(F32)
                value = jnp.where(sublane == r, -fill, value)
            picked.append(value)
        mask[x, :, tile * BLOCK : (tile + 1) * BLOCK] = by_group(picked)

    pl.semaphore_wait(barrier, len(peers))
    for level in range(1, LEVELS):
        pl.semaphore_signal(
            ready_sem.at[level], inc=1, device_id=across(level, 0), device_id_type=pl.DeviceIdType.MESH
        )

    u_copies = []
    for d in range(1, X):
        u_copies.append(remote(u_row.at[along_x(d)], u_buf.at[:, x, z], u_sem, (d - 1,), to_x(d)))
        u_copies[-1].start()

    def ring_copy(step, index, way):
        block = along_z(-way * (step - 1))
        source = along_x((0, -1, 1, 2)[index])
        if step < Z // 2:
            where = u_buf.at[:, source, block]
        else:
            where = u_buf.at[0 if way > 0 else 1, source, block]
        return remote(where, where, ring_sem, (Z * index + 2 * (step - 1) + (way < 0),), to_z(way))

    ring = {}

    def ring_step(step, index):
        if step == 1 and index:
            u_copies[(None, 0, 2, 1)[index]].wait_recv()
        for way in (1, -1):
            if step > 1:
                ring[step - 1, index, way].wait_recv()
            if step <= Z // 2:
                ring[step, index, way] = ring_copy(step, index, way)
                ring[step, index, way].start()

    ring_step(1, 0)

    def l_copy(index, source, part, d):
        where = l_buf.at[along_x(source), pl.ds(part * BLOCK, BLOCK)]
        return remote(where, where, l_sem, (index,), to_x(d))

    l_copies = [l_copy(0, 0, 0, 1), l_copy(1, 0, 1, -1), l_copy(2, 0, 1, 1), l_copy(3, 0, 0, -1)]
    for copy in l_copies:
        copy.start()
    mask_copies = []
    for d in range(1, X):
        mask_copies.append(remote(mask.at[x], mask.at[x], mask_sem, (d - 1,), to_x(d)))
        mask_copies[-1].start()

    for index in range(1, X):
        ring_step(1, index)
    for step in range(2, Z // 2 + 2):
        for index in range(X):
            ring_step(step, index)
        if step == 2:
            for index, (source, part, way) in enumerate(((-1, 0, 1), (1, 1, -1))):
                l_copies[index].wait_recv()
                l_copies.append(l_copy(4 + index, source, part, way))
                l_copies[-1].start()

    way = 1 - 2 * bit(0)
    beside, opposite = along_x(-way), along_x(2)

    sep_copies = [[] for _ in items]

    def sep_copy(i, where, sems, index, device):
        sep_copies[i].append(remote(where, where, sems, (i, index), device))
        sep_copies[i][-1].start()

    def sep_start(i):
        own_sep[i].wait()
        sep_copy(i, sep_buf.at[i, x], sep_sem, 0, to_x(way))

    def sep_forward(i):
        sep_copies[i][0].wait_recv()
        sep_copy(i, sep_buf.at[i, beside, pl.ds(bit(0) * BLOCK, BLOCK)], sep_sem, 1, to_x(way))
        sep_copy(i, sep_buf.at[i, beside], pass_sem, 0, across(0, 0))

    def sep_finish(i):
        sep_copies[i][1].wait_recv()
        sep_copy(i, sep_buf.at[i, opposite, pl.ds(bit(0) * BLOCK, BLOCK)], pass_sem, 1, across(0, 0))

    def sep_wait(i):
        sep_copies[i][2].wait_recv()
        sep_copies[i][3].wait_recv()

    for copy in mask_copies:
        copy.wait_recv()

    def weight(level, row_block):
        return jnp.where(owner_ref[node(level, 0)] == row_block * Z + z, 1.0, 0.0).astype(F32)

    core_copies = []
    y_copies = []
    order = [along_x(d) for d in (0, -1, 1, 2)]
    waits = [[], [2], [3], [4, 5]]
    giving = 1 - bit(1)
    total0 = [jnp.zeros((rows, BLOCK), F32) for _ in range(2)]
    for index in range(X + 1):
        if index < X:
            row_block = order[index]
            for which in waits[index]:
                l_copies[which].wait_recv()
            if index == X - 1:
                sep_start(0)
                sep_start(1)
            u_all = u_buf[...].reshape(panels * width, X * BLOCK)
            for r in range(rows // BLOCK):
                part = dot(l_buf[row_block, r * BLOCK : (r + 1) * BLOCK], u_all) * mask[row_block, r : r + 1]
                for h in range(2):
                    acc[h, row_block, r * BLOCK : (r + 1) * BLOCK] = part[:, h * 2 * BLOCK : (h + 1) * 2 * BLOCK]
            core_copies.append(
                remote(acc.at[1 - bit(0), row_block], other.at[row_block], core_sem, (index,), across(0, 0))
            )
            core_copies[-1].start()
        if index:
            row_block = order[index - 1]
            core_copies[index - 1].wait_recv()
            value = acc[bit(0), row_block] + other[row_block]
            for h in range(2):
                half[h, row_block] = value[:, h * BLOCK : (h + 1) * BLOCK]
                total0[h] = total0[h] + weight(0, row_block) * value[:, h * BLOCK : (h + 1) * BLOCK]
            give1[row_block] = half[giving, row_block].astype(BF16)
            y_copies.append(remote(give1.at[row_block], take1.at[row_block], y_sem, (index - 1,), across(1, 0)))
            y_copies[-1].start()

    late = []

    def each(low, act):
        def body(d, carry):
            act(d)
            return carry

        lax.fori_loop(low, Z, body, 0)

    def part_copies(level, cand, parts):
        return lambda d: remote(cand.at[along_z(d)], parts.at[d], part_sem, (level, d), to_z(d))

    def add_parts(own, parts, copies):
        def add(d, total):
            copies(d).wait_recv()
            return total + parts[d].astype(F32)

        total = lax.fori_loop(1, Z, add, own.astype(F32))
        late.append((1, copies))
        return total

    def pivot_start(level, mine, theirs, pivot):
        def here(d):
            return remote(mine, pivot.at[0, z], pivot_sem, (level, d), to_z(d))

        def there(d):
            return remote(theirs, pivot.at[1, z], pivot_sem, (level, Z + d), across(level + 1, d))

        each(1, lambda d: here(d).start())
        each(0, lambda d: there(d).start())
        pivot[0, z] = mine[...]
        return here, there

    def pivot_wait(copies):
        here, there = copies
        each(1, lambda d: here(d).wait_recv())
        each(0, lambda d: there(d).wait_recv())
        late.extend([(1, here), (0, there)])

    def update(level, row_block, pivots):
        return sum(dot(sep_buf[2 * level + i, row_block], pivot) for i, pivot in enumerate(pivots))

    for h in range(2):
        cand0[:, h] = total0[h].astype(BF16).reshape(Z, rows // Z, BLOCK)
    copies = part_copies(0, cand0, parts0)
    each(1, lambda d: copies(d).start())
    for i in (0, 1):
        sep_forward(i)
    for i in (2, 3):
        sep_start(i)
    chunk0[...] = add_parts(cand0[z], parts0, copies).astype(BF16)
    for level in range(1, LEVELS):
        pl.semaphore_wait(ready_sem.at[level], 1)
    copies = pivot_start(0, chunk0.at[bit(1)], chunk0.at[giving], pivot0)
    for i in (0, 1):
        sep_finish(i)
    for i in (2, 3):
        sep_forward(i)
    for i in (4, 5, 6):
        sep_start(i)
    for i in (0, 1):
        sep_wait(i)
    pivot_wait(copies)

    picked = jnp.zeros((rows, BLOCK), F32)
    pivots = [pivot0[i].reshape(rows, BLOCK) for i in range(2)]
    for copy in y_copies:
        copy.wait_recv()
    for row_block in range(X):
        value = half[bit(1), row_block] - update(0, row_block, pivots)
        value = value + take1[row_block].astype(F32)
        state1[row_block] = value
        picked = picked + weight(1, row_block) * value
    cand1[...] = picked.astype(BF16).reshape(Z, rows // Z, BLOCK)
    copies = part_copies(1, cand1, parts1)
    each(1, lambda d: copies(d).start())

    def pack_two(blocks, store):
        pairs = len(blocks) // 2
        for pair in range(pairs):
            low, high = blocks[pair], blocks[pair + pairs]
            store[0, pair] = by_half(low, turned(high, 2))
            store[1, pair] = by_half(turned(low, 2), high)

    pack_two([state1[row_block] for row_block in range(X)], pack2)
    give2[...] = pack2[1 - bit(2)].astype(BF16)
    y_copies.append(remote(give2, take2, y_sem, (X,), across(2, 0)))
    y_copies[-1].start()
    for i in (2, 3):
        sep_finish(i)
    for i in (2, 3):
        sep_wait(i)
    block = sum(weight(2, row_block) * sep_buf[2 + bit(0), row_block].astype(F32) for row_block in range(X))
    for h in range(2):
        corner[:, h] = block[h * BLOCK : (h + 1) * BLOCK].astype(BF16).reshape(Z, rows // Z // 2, rows)

    def corner_copies(d):
        return remote(corner.at[along_z(d)], corner_parts.at[d], corner_sem, (0, d), to_z(d))

    each(1, lambda d: corner_copies(d).start())

    chunk1[...] = add_parts(cand1[z], parts1, copies).astype(BF16)
    pivot_copies = pivot_start(1, chunk1, chunk1, pivot1)
    for i in (4, 5, 6):
        sep_forward(i)

    y_copies[-1].wait_recv()
    value = pack2[bit(2)] + take2[...].astype(F32)
    state2[...] = value
    picked = by_half(*[weight(2, 2 * h) * value[0] + weight(2, 2 * h + 1) * value[1] for h in range(2)])
    picked = picked + turned(picked, 2)
    picked = by_half(picked[: rows // 2], picked[rows // 2 :])
    cand2[...] = picked.reshape(Z, rows // Z // 2, BLOCK)
    copies = part_copies(2, cand2, parts2)
    each(1, lambda d: copies(d).start())
    mine = corner_chunk.at[bit(0)]
    corner_chunk[bit(0)] = add_parts(corner[z], corner_parts, corner_copies).astype(BF16)
    corner_pass = remote(mine, mine, corner_pass_sem, (0,), across(0, 0))
    corner_pass.start()
    corner_pass.wait_recv()
    pivot_wait(pivot_copies)

    pivots = [pivot1[i].reshape(rows, BLOCK) for i in range(2)]
    taken = sum(dot(corner_chunk[i].reshape(rows // Z, rows), pivots[i]) for i in range(2))
    pack_two([taken[: rows // Z // 2], taken[rows // Z // 2 :]], pack_chunk)
    total = add_parts(cand2[z], parts2, copies)
    chunk2[...] = (total - pack_chunk[bit(2), 0]).astype(BF16)
    pivot_copies = pivot_start(2, chunk2, chunk2, pivot2)
    pack_two([update(1, row_block, pivots) for row_block in range(X)], pack2)
    state2[...] = state2[...] - pack2[bit(2)]

    def pack_four(even, odd):
        moved_even, moved_odd = turned(even, -1), turned(odd, 1)
        pack3[0] = by_group([even, moved_odd, even, moved_odd])
        pack3[1] = by_group([moved_even, odd, moved_even, odd])

    pack_four(state2[0], state2[1])
    give3[...] = pack3[1 - bit(3)].astype(BF16)
    y_copies.append(remote(give3, take3, y_sem, (X + 1,), across(3, 0)))
    y_copies[-1].start()
    for i in (4, 5, 6):
        sep_finish(i)
    for i in (4, 5, 6):
        sep_wait(i)
    pivot_wait(pivot_copies)

    pivots = []
    for i in range(2):
        packed = pivot2[i].astype(F32).reshape(rows // 2, BLOCK)
        moved = turned(packed, 2)
        pivots.append(jnp.concatenate([by_half(packed, moved), by_half(moved, packed)], axis=0).astype(BF16))
    updates = [update(2, row_block, pivots) for row_block in range(X)]
    pack_four(*[state2[pair] - by_half(updates[pair], updates[pair + 2]) for pair in range(2)])
    y_copies[-1].wait_recv()
    value = pack3[bit(3)] + take3[...].astype(F32)
    state3[...] = value
    picked = by_group([weight(3, g) * value for g in range(X)])
    picked = picked + turned(picked, 1)
    picked = picked + turned(picked, 2)
    quarter = rows // X
    cand3[...] = by_group([picked[k * quarter : (k + 1) * quarter] for k in range(X)]).astype(BF16)

    def whole_copies(d):
        return remote(cand3, parts3.at[d], part_sem, (3, d), to_z(d))

    each(1, lambda d: whole_copies(d).start())
    packed = add_parts(cand3[...], parts3, whole_copies)
    pivot = []
    for k in range(X):
        nothing = jnp.zeros_like(packed)
        one = by_group([packed if g == k else nothing for g in range(X)])
        one = one + turned(one, 1)
        pivot.append(one + turned(one, 2))
    pivot = jnp.concatenate(pivot, axis=0).astype(BF16)
    value = state3[...] - by_group([update(3, row_block, [pivot]) for row_block in range(X)])

    for row_block in range(X):
        slices[row_block] = by_group(
            [turned(value[k * quarter : (k + 1) * quarter], k - row_block) for k in range(X)]
        )
    final_copies = []
    for d in range(1, X):
        final_copies.append(remote(slices.at[along_x(d)], final.at[x], final_sem, (d - 1,), to_x(d)))
        final_copies[-1].start()
    final[x] = slices[x]
    for copy in final_copies:
        copy.wait_recv()
    for k in range(X):
        out_ref[k * quarter : (k + 1) * quarter, :] = by_group([turned(final[q], q - k) for q in range(X)])

    started = [corner_pass] + u_copies + mask_copies + l_copies + list(ring.values()) + core_copies + y_copies + final_copies
    for copy in started + [copy for item in sep_copies for copy in item]:
        copy.wait_send()
    for low, copies in late:
        each(low, lambda d, copies=copies: copies(d).wait_send())


def local(l_panels, u_panels, panel_fill, copy_fill, sep_panels, sep_owner):
    _, panels, rows, width = l_panels.shape
    depth, columns = u_panels.shape[2:]
    quarter = columns // X
    items = 2 * LEVELS - 1
    remote_sems = [
        (X - 1,), (X - 1,), (6,), (X * Z,), (X,), (items, 2), (items, 2), None, (X + 2,), (LEVELS, Z),
        (LEVELS - 1, 2 * Z), (X - 1,), (1, Z), (1,),
    ]
    chunk = rows // Z
    kept = pl.BlockSpec(memory_space=pl.ANY)
    return pl.pallas_call(
        kernel,
        out_shape=jax.ShapeDtypeStruct((rows, BLOCK), F32),
        in_specs=[kept] * 6,
        out_specs=pl.BlockSpec(memory_space=pltpu.VMEM),
        scratch_shapes=[
            pltpu.SMEM(sep_owner.shape, jnp.int32),
            pltpu.SMEM(panel_fill.shape, jnp.int32),
            pltpu.SMEM(copy_fill.shape, jnp.int32),
            pltpu.VMEM(l_panels.shape, BF16),
            pltpu.VMEM(u_panels.shape, BF16),
            pltpu.VMEM((X, panels, depth, quarter), BF16),
            pltpu.VMEM((panels, X, Z, depth, quarter), BF16),
            pltpu.VMEM((X, rows, panels * width), BF16),
            pltpu.VMEM((X, 8, quarter), F32),
            pltpu.VMEM((2, X, rows, 2 * BLOCK), F32),
            pltpu.VMEM((X, rows, 2 * BLOCK), F32),
            pltpu.VMEM((2, X, rows, BLOCK), F32),
            pltpu.VMEM((items, X, rows, sep_panels.shape[2]), BF16),
            pltpu.VMEM((X, rows, BLOCK), BF16),
            pltpu.VMEM((X, rows, BLOCK), BF16),
            pltpu.VMEM((X, rows, BLOCK), F32),
            pltpu.VMEM((2, 2, rows, BLOCK), F32),
            pltpu.VMEM((2, rows, BLOCK), BF16),
            pltpu.VMEM((2, rows, BLOCK), BF16),
            pltpu.VMEM((2, rows, BLOCK), F32),
            pltpu.VMEM((2, rows, BLOCK), F32),
            pltpu.VMEM((rows, BLOCK), BF16),
            pltpu.VMEM((rows, BLOCK), BF16),
            pltpu.VMEM((rows, BLOCK), F32),
            pltpu.VMEM((Z, 2, chunk, BLOCK), BF16),
            pltpu.VMEM((Z, 2, chunk, BLOCK), BF16),
            pltpu.VMEM((2, chunk, BLOCK), BF16),
            pltpu.VMEM((2, Z, chunk, BLOCK), BF16),
            pltpu.VMEM((Z, chunk, BLOCK), BF16),
            pltpu.VMEM((Z, chunk, BLOCK), BF16),
            pltpu.VMEM((chunk, BLOCK), BF16),
            pltpu.VMEM((2, Z, chunk, BLOCK), BF16),
            pltpu.VMEM((Z, chunk // 2, BLOCK), F32),
            pltpu.VMEM((Z, chunk // 2, BLOCK), F32),
            pltpu.VMEM((chunk // 2, BLOCK), BF16),
            pltpu.VMEM((2, Z, chunk // 2, BLOCK), BF16),
            pltpu.VMEM((rows // X, BLOCK), BF16),
            pltpu.VMEM((Z, rows // X, BLOCK), BF16),
            pltpu.VMEM((X, rows // X, BLOCK), F32),
            pltpu.VMEM((X, rows // X, BLOCK), F32),
            pltpu.VMEM((Z, 2, chunk // 2, rows), BF16),
            pltpu.VMEM((Z, 2, chunk // 2, rows), BF16),
            pltpu.VMEM((2, 2, chunk // 2, rows), BF16),
            pltpu.VMEM((2, 1, chunk // 2, BLOCK), F32),
            *[pltpu.SemaphoreType.DMA((items + 5,) if s is None else (2, *s)) for s in remote_sems],
            pltpu.SemaphoreType.REGULAR((LEVELS,)),
        ],
        compiler_params=pltpu.CompilerParams(
            collective_id=0, has_side_effects=True, vmem_limit_bytes=60 * 2**20
        ),
        cost_estimate=pl.CostEstimate(flops=2**31, bytes_accessed=2**22, transcendentals=0),
    )(sep_owner, panel_fill, copy_fill, l_panels, u_panels, sep_panels)


def solution(mesh):
    return jax.shard_map(
        local,
        mesh=mesh,
        in_specs=(
            P("layer", None, "grid", None),
            P("layer", None, "grid", None),
            P("layer", None, "grid", None),
            P("layer", "grid", None),
            P(None, "grid", None),
            P(),
        ),
        out_specs=P("grid", "layer"),
        check_vma=False,
    )
```

```python
import jax
import jax.numpy as jnp
from jax import lax
from jax.experimental import pallas as pl
from jax.experimental.pallas import tpu as pltpu
from jax.sharding import PartitionSpec as P

BLOCK = 128
X = 4
Z = 8
GROUP = BLOCK // X
LEVELS = 4
F32 = jnp.float32
BF16 = jnp.bfloat16


def turned(v, groups):
    shift = groups % X * GROUP
    return pltpu.roll(v, shift, 1) if shift else v


def by_group(pieces):
    group = lax.broadcasted_iota(jnp.int32, pieces[0].shape, 1) // GROUP
    out = pieces[0]
    for g in range(1, X):
        out = jnp.where(group == g, pieces[g], out)
    return out


def by_half(low, high):
    lane = lax.broadcasted_iota(jnp.int32, low.shape, 1)
    return jnp.where(lane < BLOCK // 2, low, high)


def column_block(tile, group):
    return (tile >> 1) + 2 * (tile & 1) + 4 * (group >> 1) + 8 * (group & 1)


def dot(a, b):
    return jnp.dot(a, b, preferred_element_type=F32)


def kernel(
    owner_any, panel_fill_any, copy_fill_any, l_any, u_any, sep_ref, out_ref,
    owner_ref, panel_fill_ref, copy_fill_ref, l_ref, u_ref,
    u_row, u_buf, l_buf, mask, acc, other, half, sep_buf,
    give1, take1, state1, pack2, give2, take2, state2, pack3, give3, take3, state3,
    cand0, parts0, chunk0, pivot0, cand1, parts1, chunk1, pivot1, cand2, parts2, chunk2, pivot2, cand3, parts3,
    slices, final, corner, corner_parts, corner_chunk, pack_chunk,
    u_sem, mask_sem, l_sem, ring_sem, core_sem, sep_sem, pass_sem, own_sem, y_sem, part_sem, pivot_sem, final_sem,
    corner_sem, corner_pass_sem, ready_sem,
):
    layer = lax.axis_index("layer")
    grid = lax.axis_index("grid")
    x = grid // Z
    z = grid % Z
    rows = l_ref.shape[2]
    width = l_ref.shape[3]
    panels = l_ref.shape[1]
    depth = u_ref.shape[2]

    def along_x(d):
        return (x + d) % X

    def along_z(d):
        return (z + d) % Z

    def bit(level):
        return layer // 2**level % 2

    def partner(level):
        return layer + 2**level * (1 - 2 * bit(level))

    def remote(src, dst, sems, index, device):
        return pltpu.make_async_remote_copy(
            src_ref=src,
            dst_ref=dst,
            send_sem=sems.at[(0, *index)],
            recv_sem=sems.at[(1, *index)],
            device_id=device,
            device_id_type=pl.DeviceIdType.MESH,
        )

    def to_x(d):
        return {"grid": along_x(d) * Z + z}

    def to_z(d):
        return {"grid": x * Z + along_z(d)}

    def across(level, d):
        return {"layer": partner(level), "grid": x * Z + along_z(d)}

    def node(level, sibling):
        group = layer // 2 ** (level + 1)
        if sibling:
            group = group + 1 - 2 * (group % 2)
        return 2**LEVELS - (2**LEVELS >> level) + group

    barrier = pltpu.get_barrier_semaphore()
    peers = [to_x(d) for d in range(1, X)] + [to_z(d) for d in range(1, Z)]
    peers += [across(level, 0) for level in range(LEVELS)]
    for peer in peers:
        pl.semaphore_signal(barrier, inc=1, device_id=peer, device_id_type=pl.DeviceIdType.MESH)

    pairs = ((u_any, u_ref), (panel_fill_any, panel_fill_ref), (l_any, l_ref), (copy_fill_any, copy_fill_ref), (owner_any, owner_ref))
    loads = [pltpu.make_async_copy(src, dst, own_sem.at[i]) for i, (src, dst) in enumerate(pairs)]
    for load in loads:
        load.start()
    load_u, load_panel_fill, load_l, load_copy_fill, load_owner = loads
    items = [(level, sibling) for level in range(LEVELS) for sibling in range(2)][:-1]
    own_sep = []
    for i, (level, sibling) in enumerate(items):
        own_sep.append(
            pltpu.make_async_copy(sep_ref.at[node(level, sibling)], sep_buf.at[i, x], own_sem.at[len(loads) + i])
        )
        own_sep[i].start()

    load_u.wait()
    turns = {}
    for tile in range(X):
        for group in range(X):
            block = column_block(tile, group)
            piece = u_ref[0, :, :, block * BLOCK : (block + 1) * BLOCK].astype(F32).reshape(panels * depth, BLOCK)
            turns[tile, group] = [turned(piece, n) for n in range(X)]
        for quarter in range(X):
            mixed = by_group([turns[tile, group][(group - quarter) % X] for group in range(X)])
            u_row[quarter, :, :, tile * BLOCK : (tile + 1) * BLOCK] = mixed.astype(BF16).reshape(panels, depth, BLOCK)
    u_buf[:, x, z] = u_row[x]

    load_panel_fill.wait()
    load_l.wait()
    for r in range(rows // BLOCK):
        for k in range(panels):
            for c in range(width // BLOCK):
                fill = panel_fill_ref[0, k, r, c].astype(F32)
                piece = l_ref[0, k, r * BLOCK : (r + 1) * BLOCK, c * BLOCK : (c + 1) * BLOCK].astype(F32) * fill
                l_buf[x, r * BLOCK : (r + 1) * BLOCK, k * width + c * BLOCK : k * width + (c + 1) * BLOCK] = (
                    piece.astype(BF16)
                )

    load_copy_fill.wait()
    load_owner.wait()
    shape = (8, BLOCK)
    sublane = lax.broadcasted_iota(jnp.int32, shape, 0)
    for tile in range(X):
        picked = []
        for group in range(X):
            value = jnp.zeros(shape, F32)
            for r in range(rows // BLOCK):
                fill = copy_fill_ref[0, r, column_block(tile, group)].astype(F32)
                value = jnp.where(sublane == r, -fill, value)
            picked.append(value)
        mask[x, :, tile * BLOCK : (tile + 1) * BLOCK] = by_group(picked)

    pl.semaphore_wait(barrier, len(peers))
    for level in range(1, LEVELS):
        pl.semaphore_signal(
            ready_sem.at[level], inc=1, device_id=across(level, 0), device_id_type=pl.DeviceIdType.MESH
        )

    u_copies = []
    for d in range(1, X):
        u_copies.append(remote(u_row.at[along_x(d)], u_buf.at[:, x, z], u_sem, (d - 1,), to_x(d)))
        u_copies[-1].start()

    def ring_copy(step, index, way):
        block = along_z(-way * (step - 1))
        source = along_x((0, -1, 1, 2)[index])
        if step < Z // 2:
            where = u_buf.at[:, source, block]
        else:
            where = u_buf.at[0 if way > 0 else 1, source, block]
        return remote(where, where, ring_sem, (Z * index + 2 * (step - 1) + (way < 0),), to_z(way))

    ring = {}

    def ring_step(step, index):
        if step == 1 and index:
            u_copies[(None, 0, 2, 1)[index]].wait_recv()
        for way in (1, -1):
            if step > 1:
                ring[step - 1, index, way].wait_recv()
            if step <= Z // 2:
                ring[step, index, way] = ring_copy(step, index, way)
                ring[step, index, way].start()

    ring_step(1, 0)

    def l_copy(index, source, part, d):
        where = l_buf.at[along_x(source), pl.ds(part * BLOCK, BLOCK)]
        return remote(where, where, l_sem, (index,), to_x(d))

    l_copies = [l_copy(0, 0, 0, 1), l_copy(1, 0, 1, -1), l_copy(2, 0, 1, 1), l_copy(3, 0, 0, -1)]
    for copy in l_copies:
        copy.start()
    mask_copies = []
    for d in range(1, X):
        mask_copies.append(remote(mask.at[x], mask.at[x], mask_sem, (d - 1,), to_x(d)))
        mask_copies[-1].start()

    for index in range(1, X):
        ring_step(1, index)
    for step in range(2, Z // 2 + 2):
        for index in range(X):
            ring_step(step, index)
        if step == 2:
            for index, (source, part, way) in enumerate(((-1, 0, 1), (1, 1, -1))):
                l_copies[index].wait_recv()
                l_copies.append(l_copy(4 + index, source, part, way))
                l_copies[-1].start()

    way = 1 - 2 * bit(0)
    beside, opposite = along_x(-way), along_x(2)

    sep_copies = [[] for _ in items]

    def sep_copy(i, where, sems, index, device):
        sep_copies[i].append(remote(where, where, sems, (i, index), device))
        sep_copies[i][-1].start()

    def sep_start(i):
        own_sep[i].wait()
        sep_copy(i, sep_buf.at[i, x], sep_sem, 0, to_x(way))

    def sep_forward(i):
        sep_copies[i][0].wait_recv()
        sep_copy(i, sep_buf.at[i, beside, pl.ds(bit(0) * BLOCK, BLOCK)], sep_sem, 1, to_x(way))
        sep_copy(i, sep_buf.at[i, beside], pass_sem, 0, across(0, 0))

    def sep_finish(i):
        sep_copies[i][1].wait_recv()
        sep_copy(i, sep_buf.at[i, opposite, pl.ds(bit(0) * BLOCK, BLOCK)], pass_sem, 1, across(0, 0))

    def sep_wait(i):
        sep_copies[i][2].wait_recv()
        sep_copies[i][3].wait_recv()

    for copy in mask_copies:
        copy.wait_recv()

    def weight(level, row_block):
        return jnp.where(owner_ref[node(level, 0)] == row_block * Z + z, 1.0, 0.0).astype(F32)

    core_copies = []
    y_copies = []
    order = [along_x(d) for d in (0, -1, 1, 2)]
    waits = [[], [2], [3], [4, 5]]
    giving = 1 - bit(1)
    total0 = [jnp.zeros((rows, BLOCK), F32) for _ in range(2)]
    for index in range(X + 1):
        if index < X:
            row_block = order[index]
            for which in waits[index]:
                l_copies[which].wait_recv()
            if index == X - 1:
                sep_start(0)
                sep_start(1)
            u_all = u_buf[...].reshape(panels * width, X * BLOCK)
            for r in range(rows // BLOCK):
                part = dot(l_buf[row_block, r * BLOCK : (r + 1) * BLOCK], u_all) * mask[row_block, r : r + 1]
                for h in range(2):
                    acc[h, row_block, r * BLOCK : (r + 1) * BLOCK] = part[:, h * 2 * BLOCK : (h + 1) * 2 * BLOCK]
            core_copies.append(
                remote(acc.at[1 - bit(0), row_block], other.at[row_block], core_sem, (index,), across(0, 0))
            )
            core_copies[-1].start()
        if index:
            row_block = order[index - 1]
            core_copies[index - 1].wait_recv()
            value = acc[bit(0), row_block] + other[row_block]
            for h in range(2):
                half[h, row_block] = value[:, h * BLOCK : (h + 1) * BLOCK]
                total0[h] = total0[h] + weight(0, row_block) * value[:, h * BLOCK : (h + 1) * BLOCK]
            give1[row_block] = half[giving, row_block].astype(BF16)
            y_copies.append(remote(give1.at[row_block], take1.at[row_block], y_sem, (index - 1,), across(1, 0)))
            y_copies[-1].start()

    late = []

    def each(low, act):
        for d in range(low, Z):
            act(d)

    def part_copies(level, cand, parts):
        return lambda d: remote(cand.at[along_z(d)], parts.at[d], part_sem, (level, d), to_z(d))

    def add_parts(own, parts, copies):
        total = own.astype(F32)
        for d in range(1, Z):
            copies(d).wait_recv()
            total = total + parts[d].astype(F32)
        late.append((1, copies))
        return total

    def pivot_start(level, mine, theirs, pivot):
        def here(d):
            return remote(mine, pivot.at[0, z], pivot_sem, (level, d), to_z(d))

        def there(d):
            return remote(theirs, pivot.at[1, z], pivot_sem, (level, Z + d), across(level + 1, d))

        each(1, lambda d: here(d).start())
        each(0, lambda d: there(d).start())
        pivot[0, z] = mine[...]
        return here, there

    def pivot_wait(copies):
        here, there = copies
        each(1, lambda d: here(d).wait_recv())
        each(0, lambda d: there(d).wait_recv())
        late.extend([(1, here), (0, there)])

    def update(level, row_block, pivots):
        return sum(dot(sep_buf[2 * level + i, row_block], pivot) for i, pivot in enumerate(pivots))

    for h in range(2):
        cand0[:, h] = total0[h].astype(BF16).reshape(Z, rows // Z, BLOCK)
    copies = part_copies(0, cand0, parts0)
    each(1, lambda d: copies(d).start())
    for i in (0, 1):
        sep_forward(i)
    for i in (2, 3):
        sep_start(i)
    chunk0[...] = add_parts(cand0[z], parts0, copies).astype(BF16)
    for level in range(1, LEVELS):
        pl.semaphore_wait(ready_sem.at[level], 1)
    copies = pivot_start(0, chunk0.at[bit(1)], chunk0.at[giving], pivot0)
    for i in (0, 1):
        sep_finish(i)
    for i in (2, 3):
        sep_forward(i)
    for i in (4, 5, 6):
        sep_start(i)
    for i in (0, 1):
        sep_wait(i)
    pivot_wait(copies)

    picked = jnp.zeros((rows, BLOCK), F32)
    pivots = [pivot0[i].reshape(rows, BLOCK) for i in range(2)]
    for copy in y_copies:
        copy.wait_recv()
    for row_block in range(X):
        value = half[bit(1), row_block] - update(0, row_block, pivots)
        value = value + take1[row_block].astype(F32)
        state1[row_block] = value
        picked = picked + weight(1, row_block) * value
    cand1[...] = picked.astype(BF16).reshape(Z, rows // Z, BLOCK)
    copies = part_copies(1, cand1, parts1)
    each(1, lambda d: copies(d).start())

    def pack_two(blocks, store):
        pairs = len(blocks) // 2
        for pair in range(pairs):
            low, high = blocks[pair], blocks[pair + pairs]
            store[0, pair] = by_half(low, turned(high, 2))
            store[1, pair] = by_half(turned(low, 2), high)

    pack_two([state1[row_block] for row_block in range(X)], pack2)
    give2[...] = pack2[1 - bit(2)].astype(BF16)
    y_copies.append(remote(give2, take2, y_sem, (X,), across(2, 0)))
    y_copies[-1].start()
    for i in (2, 3):
        sep_finish(i)
    for i in (2, 3):
        sep_wait(i)
    block = sum(weight(2, row_block) * sep_buf[2 + bit(0), row_block].astype(F32) for row_block in range(X))
    for h in range(2):
        corner[:, h] = block[h * BLOCK : (h + 1) * BLOCK].astype(BF16).reshape(Z, rows // Z // 2, rows)

    def corner_copies(d):
        return remote(corner.at[along_z(d)], corner_parts.at[d], corner_sem, (0, d), to_z(d))

    each(1, lambda d: corner_copies(d).start())

    chunk1[...] = add_parts(cand1[z], parts1, copies).astype(BF16)
    pivot_copies = pivot_start(1, chunk1, chunk1, pivot1)
    for i in (4, 5, 6):
        sep_forward(i)

    y_copies[-1].wait_recv()
    value = pack2[bit(2)] + take2[...].astype(F32)
    state2[...] = value
    picked = by_half(*[weight(2, 2 * h) * value[0] + weight(2, 2 * h + 1) * value[1] for h in range(2)])
    picked = picked + turned(picked, 2)
    picked = by_half(picked[: rows // 2], picked[rows // 2 :])
    cand2[...] = picked.reshape(Z, rows // Z // 2, BLOCK)
    copies = part_copies(2, cand2, parts2)
    each(1, lambda d: copies(d).start())
    mine = corner_chunk.at[bit(0)]
    corner_chunk[bit(0)] = add_parts(corner[z], corner_parts, corner_copies).astype(BF16)
    corner_pass = remote(mine, mine, corner_pass_sem, (0,), across(0, 0))
    corner_pass.start()
    corner_pass.wait_recv()
    pivot_wait(pivot_copies)

    pivots = [pivot1[i].reshape(rows, BLOCK) for i in range(2)]
    taken = sum(dot(corner_chunk[i].reshape(rows // Z, rows), pivots[i]) for i in range(2))
    pack_two([taken[: rows // Z // 2], taken[rows // Z // 2 :]], pack_chunk)
    total = add_parts(cand2[z], parts2, copies)
    chunk2[...] = (total - pack_chunk[bit(2), 0]).astype(BF16)
    pivot_copies = pivot_start(2, chunk2, chunk2, pivot2)
    pack_two([update(1, row_block, pivots) for row_block in range(X)], pack2)
    state2[...] = state2[...] - pack2[bit(2)]

    def pack_four(even, odd):
        moved_even, moved_odd = turned(even, -1), turned(odd, 1)
        pack3[0] = by_group([even, moved_odd, even, moved_odd])
        pack3[1] = by_group([moved_even, odd, moved_even, odd])

    pack_four(state2[0], state2[1])
    give3[...] = pack3[1 - bit(3)].astype(BF16)
    y_copies.append(remote(give3, take3, y_sem, (X + 1,), across(3, 0)))
    y_copies[-1].start()
    for i in (4, 5, 6):
        sep_finish(i)
    for i in (4, 5, 6):
        sep_wait(i)
    pivot_wait(pivot_copies)

    pivots = []
    for i in range(2):
        packed = pivot2[i].astype(F32).reshape(rows // 2, BLOCK)
        moved = turned(packed, 2)
        pivots.append(jnp.concatenate([by_half(packed, moved), by_half(moved, packed)], axis=0).astype(BF16))
    updates = [update(2, row_block, pivots) for row_block in range(X)]
    pack_four(*[state2[pair] - by_half(updates[pair], updates[pair + 2]) for pair in range(2)])
    y_copies[-1].wait_recv()
    value = pack3[bit(3)] + take3[...].astype(F32)
    state3[...] = value
    picked = by_group([weight(3, g) * value for g in range(X)])
    picked = picked + turned(picked, 1)
    picked = picked + turned(picked, 2)
    quarter = rows // X
    cand3[...] = by_group([picked[k * quarter : (k + 1) * quarter] for k in range(X)]).astype(BF16)

    def whole_copies(d):
        return remote(cand3, parts3.at[d], part_sem, (3, d), to_z(d))

    each(1, lambda d: whole_copies(d).start())
    packed = add_parts(cand3[...], parts3, whole_copies)
    pivot = []
    for k in range(X):
        nothing = jnp.zeros_like(packed)
        one = by_group([packed if g == k else nothing for g in range(X)])
        one = one + turned(one, 1)
        pivot.append(one + turned(one, 2))
    pivot = jnp.concatenate(pivot, axis=0).astype(BF16)
    value = state3[...] - by_group([update(3, row_block, [pivot]) for row_block in range(X)])

    for row_block in range(X):
        slices[row_block] = by_group(
            [turned(value[k * quarter : (k + 1) * quarter], k - row_block) for k in range(X)]
        )
    final_copies = []
    for d in range(1, X):
        final_copies.append(remote(slices.at[along_x(d)], final.at[x], final_sem, (d - 1,), to_x(d)))
        final_copies[-1].start()
    final[x] = slices[x]
    for copy in final_copies:
        copy.wait_recv()
    for k in range(X):
        out_ref[k * quarter : (k + 1) * quarter, :] = by_group([turned(final[q], q - k) for q in range(X)])

    started = [corner_pass] + u_copies + mask_copies + l_copies + list(ring.values()) + core_copies + y_copies + final_copies
    for copy in started + [copy for item in sep_copies for copy in item]:
        copy.wait_send()
    for low, copies in late:
        each(low, lambda d, copies=copies: copies(d).wait_send())


def local(l_panels, u_panels, panel_fill, copy_fill, sep_panels, sep_owner):
    _, panels, rows, width = l_panels.shape
    depth, columns = u_panels.shape[2:]
    quarter = columns // X
    items = 2 * LEVELS - 1
    remote_sems = [
        (X - 1,), (X - 1,), (6,), (X * Z,), (X,), (items, 2), (items, 2), None, (X + 2,), (LEVELS, Z),
        (LEVELS - 1, 2 * Z), (X - 1,), (1, Z), (1,),
    ]
    chunk = rows // Z
    kept = pl.BlockSpec(memory_space=pl.ANY)
    return pl.pallas_call(
        kernel,
        out_shape=jax.ShapeDtypeStruct((rows, BLOCK), F32),
        in_specs=[kept] * 6,
        out_specs=pl.BlockSpec(memory_space=pltpu.VMEM),
        scratch_shapes=[
            pltpu.SMEM(sep_owner.shape, jnp.int32),
            pltpu.SMEM(panel_fill.shape, jnp.int32),
            pltpu.SMEM(copy_fill.shape, jnp.int32),
            pltpu.VMEM(l_panels.shape, BF16),
            pltpu.VMEM(u_panels.shape, BF16),
            pltpu.VMEM((X, panels, depth, quarter), BF16),
            pltpu.VMEM((panels, X, Z, depth, quarter), BF16),
            pltpu.VMEM((X, rows, panels * width), BF16),
            pltpu.VMEM((X, 8, quarter), F32),
            pltpu.VMEM((2, X, rows, 2 * BLOCK), F32),
            pltpu.VMEM((X, rows, 2 * BLOCK), F32),
            pltpu.VMEM((2, X, rows, BLOCK), F32),
            pltpu.VMEM((items, X, rows, sep_panels.shape[2]), BF16),
            pltpu.VMEM((X, rows, BLOCK), BF16),
            pltpu.VMEM((X, rows, BLOCK), BF16),
            pltpu.VMEM((X, rows, BLOCK), F32),
            pltpu.VMEM((2, 2, rows, BLOCK), F32),
            pltpu.VMEM((2, rows, BLOCK), BF16),
            pltpu.VMEM((2, rows, BLOCK), BF16),
            pltpu.VMEM((2, rows, BLOCK), F32),
            pltpu.VMEM((2, rows, BLOCK), F32),
            pltpu.VMEM((rows, BLOCK), BF16),
            pltpu.VMEM((rows, BLOCK), BF16),
            pltpu.VMEM((rows, BLOCK), F32),
            pltpu.VMEM((Z, 2, chunk, BLOCK), BF16),
            pltpu.VMEM((Z, 2, chunk, BLOCK), BF16),
            pltpu.VMEM((2, chunk, BLOCK), BF16),
            pltpu.VMEM((2, Z, chunk, BLOCK), BF16),
            pltpu.VMEM((Z, chunk, BLOCK), BF16),
            pltpu.VMEM((Z, chunk, BLOCK), BF16),
            pltpu.VMEM((chunk, BLOCK), BF16),
            pltpu.VMEM((2, Z, chunk, BLOCK), BF16),
            pltpu.VMEM((Z, chunk // 2, BLOCK), F32),
            pltpu.VMEM((Z, chunk // 2, BLOCK), F32),
            pltpu.VMEM((chunk // 2, BLOCK), BF16),
            pltpu.VMEM((2, Z, chunk // 2, BLOCK), BF16),
            pltpu.VMEM((rows // X, BLOCK), BF16),
            pltpu.VMEM((Z, rows // X, BLOCK), BF16),
            pltpu.VMEM((X, rows // X, BLOCK), F32),
            pltpu.VMEM((X, rows // X, BLOCK), F32),
            pltpu.VMEM((Z, 2, chunk // 2, rows), BF16),
            pltpu.VMEM((Z, 2, chunk // 2, rows), BF16),
            pltpu.VMEM((2, 2, chunk // 2, rows), BF16),
            pltpu.VMEM((2, 1, chunk // 2, BLOCK), F32),
            *[pltpu.SemaphoreType.DMA((items + 5,) if s is None else (2, *s)) for s in remote_sems],
            pltpu.SemaphoreType.REGULAR((LEVELS,)),
        ],
        compiler_params=pltpu.CompilerParams(
            collective_id=0, has_side_effects=True, vmem_limit_bytes=60 * 2**20
        ),
        cost_estimate=pl.CostEstimate(flops=2**31, bytes_accessed=2**22, transcendentals=0),
    )(sep_owner, panel_fill, copy_fill, l_panels, u_panels, sep_panels)


def solution(mesh):
    return jax.shard_map(
        local,
        mesh=mesh,
        in_specs=(
            P("layer", None, "grid", None),
            P("layer", None, "grid", None),
            P("layer", None, "grid", None),
            P("layer", "grid", None),
            P(None, "grid", None),
            P(),
        ),
        out_specs=P("grid", "layer"),
        check_vma=False,
    )
```

```python
import jax
import jax.numpy as jnp
from jax import lax
from jax.experimental import pallas as pl
from jax.experimental.pallas import tpu as pltpu
from jax.sharding import PartitionSpec as P

BLOCK = 128
X = 4
Z = 8
GROUP = BLOCK // X
LEVELS = 4
F32 = jnp.float32
BF16 = jnp.bfloat16


def turned(v, groups):
    shift = groups % X * GROUP
    return pltpu.roll(v, shift, 1) if shift else v


def by_group(pieces):
    group = lax.broadcasted_iota(jnp.int32, pieces[0].shape, 1) // GROUP
    out = pieces[0]
    for g in range(1, X):
        out = jnp.where(group == g, pieces[g], out)
    return out


def by_half(low, high):
    lane = lax.broadcasted_iota(jnp.int32, low.shape, 1)
    return jnp.where(lane < BLOCK // 2, low, high)


def column_block(tile, group):
    return (tile >> 1) + 2 * (tile & 1) + 4 * (group >> 1) + 8 * (group & 1)


def dot(a, b):
    return jnp.dot(a, b, preferred_element_type=F32)


def kernel(
    owner_any, panel_fill_any, copy_fill_any, l_any, u_any, sep_ref, out_ref,
    owner_ref, panel_fill_ref, copy_fill_ref, l_ref, u_ref,
    u_row, u_buf, l_buf, mask, acc, other, half, sep_buf,
    give1, take1, state1, pack2, give2, take2, state2, pack3, give3, take3, state3,
    cand0, parts0, chunk0, pivot0, cand1, parts1, chunk1, pivot1, cand2, parts2, chunk2, pivot2, cand3, parts3,
    slices, final, corner, corner_parts, corner_chunk, pack_chunk,
    u_sem, mask_sem, l_sem, ring_sem, core_sem, sep_sem, pass_sem, own_sem, y_sem, part_sem, pivot_sem, final_sem,
    corner_sem, corner_pass_sem, ready_sem,
):
    layer = lax.axis_index("layer")
    grid = lax.axis_index("grid")
    x = grid // Z
    z = grid % Z
    rows = l_ref.shape[2]
    width = l_ref.shape[3]
    panels = l_ref.shape[1]
    depth = u_ref.shape[2]

    def along_x(d):
        return (x + d) % X

    def along_z(d):
        return (z + d) % Z

    def bit(level):
        return layer // 2**level % 2

    def partner(level):
        return layer + 2**level * (1 - 2 * bit(level))

    def remote(src, dst, sems, index, device):
        return pltpu.make_async_remote_copy(
            src_ref=src,
            dst_ref=dst,
            send_sem=sems.at[(0, *index)],
            recv_sem=sems.at[(1, *index)],
            device_id=device,
            device_id_type=pl.DeviceIdType.MESH,
        )

    def to_x(d):
        return {"grid": along_x(d) * Z + z}

    def to_z(d):
        return {"grid": x * Z + along_z(d)}

    def across(level, d):
        return {"layer": partner(level), "grid": x * Z + along_z(d)}

    def node(level, sibling):
        group = layer // 2 ** (level + 1)
        if sibling:
            group = group + 1 - 2 * (group % 2)
        return 2**LEVELS - (2**LEVELS >> level) + group

    barrier = pltpu.get_barrier_semaphore()
    peers = [to_x(d) for d in range(1, X)] + [to_z(d) for d in range(1, Z)]
    peers += [across(level, 0) for level in range(LEVELS)]
    for peer in peers:
        pl.semaphore_signal(barrier, inc=1, device_id=peer, device_id_type=pl.DeviceIdType.MESH)

    pairs = ((u_any, u_ref), (panel_fill_any, panel_fill_ref), (l_any, l_ref), (copy_fill_any, copy_fill_ref), (owner_any, owner_ref))
    loads = [pltpu.make_async_copy(src, dst, own_sem.at[i]) for i, (src, dst) in enumerate(pairs)]
    for load in loads:
        load.start()
    load_u, load_panel_fill, load_l, load_copy_fill, load_owner = loads
    items = [(level, sibling) for level in range(LEVELS) for sibling in range(2)][:-1]
    own_sep = []
    for i, (level, sibling) in enumerate(items):
        own_sep.append(
            pltpu.make_async_copy(sep_ref.at[node(level, sibling)], sep_buf.at[i, x], own_sem.at[len(loads) + i])
        )
        own_sep[i].start()

    load_u.wait()
    turns = {}
    for tile in range(X):
        for group in range(X):
            block = column_block(tile, group)
            piece = u_ref[0, :, :, block * BLOCK : (block + 1) * BLOCK].astype(F32).reshape(panels * depth, BLOCK)
            turns[tile, group] = [turned(piece, n) for n in range(X)]
        for quarter in range(X):
            mixed = by_group([turns[tile, group][(group - quarter) % X] for group in range(X)])
            u_row[quarter, :, :, tile * BLOCK : (tile + 1) * BLOCK] = mixed.astype(BF16).reshape(panels, depth, BLOCK)
    u_buf[:, x, z] = u_row[x]

    load_panel_fill.wait()
    load_l.wait()
    for r in range(rows // BLOCK):
        for k in range(panels):
            for c in range(width // BLOCK):
                fill = panel_fill_ref[0, k, r, c].astype(F32)
                piece = l_ref[0, k, r * BLOCK : (r + 1) * BLOCK, c * BLOCK : (c + 1) * BLOCK].astype(F32) * fill
                l_buf[x, r * BLOCK : (r + 1) * BLOCK, k * width + c * BLOCK : k * width + (c + 1) * BLOCK] = (
                    piece.astype(BF16)
                )

    load_copy_fill.wait()
    load_owner.wait()
    shape = (8, BLOCK)
    sublane = lax.broadcasted_iota(jnp.int32, shape, 0)
    for tile in range(X):
        picked = []
        for group in range(X):
            value = jnp.zeros(shape, F32)
            for r in range(rows // BLOCK):
                fill = copy_fill_ref[0, r, column_block(tile, group)].astype(F32)
                value = jnp.where(sublane == r, -fill, value)
            picked.append(value)
        mask[x, :, tile * BLOCK : (tile + 1) * BLOCK] = by_group(picked)

    pl.semaphore_wait(barrier, len(peers))
    for level in range(1, LEVELS):
        pl.semaphore_signal(
            ready_sem.at[level], inc=1, device_id=across(level, 0), device_id_type=pl.DeviceIdType.MESH
        )

    u_copies = []
    for d in range(1, X):
        u_copies.append(remote(u_row.at[along_x(d)], u_buf.at[:, x, z], u_sem, (d - 1,), to_x(d)))
        u_copies[-1].start()

    def ring_copy(step, index, way):
        block = along_z(-way * (step - 1))
        source = along_x((0, -1, 1, 2)[index])
        if step < Z // 2:
            where = u_buf.at[:, source, block]
        else:
            where = u_buf.at[0 if way > 0 else 1, source, block]
        return remote(where, where, ring_sem, (Z * index + 2 * (step - 1) + (way < 0),), to_z(way))

    ring = {}

    def ring_step(step, index):
        if step == 1 and index:
            u_copies[(None, 0, 2, 1)[index]].wait_recv()
        for way in (1, -1):
            if step > 1:
                ring[step - 1, index, way].wait_recv()
            if step <= Z // 2:
                ring[step, index, way] = ring_copy(step, index, way)
                ring[step, index, way].start()

    ring_step(1, 0)

    def l_copy(index, source, part, d):
        where = l_buf.at[along_x(source), pl.ds(part * BLOCK, BLOCK)]
        return remote(where, where, l_sem, (index,), to_x(d))

    l_copies = [l_copy(0, 0, 0, 1), l_copy(1, 0, 1, -1), l_copy(2, 0, 1, 1), l_copy(3, 0, 0, -1)]
    for copy in l_copies:
        copy.start()
    mask_copies = []
    for d in range(1, X):
        mask_copies.append(remote(mask.at[x], mask.at[x], mask_sem, (d - 1,), to_x(d)))
        mask_copies[-1].start()

    for index in range(1, X):
        ring_step(1, index)
    for step in range(2, Z // 2 + 2):
        for index in range(X):
            ring_step(step, index)
        if step == 2:
            for index, (source, part, way) in enumerate(((-1, 0, 1), (1, 1, -1))):
                l_copies[index].wait_recv()
                l_copies.append(l_copy(4 + index, source, part, way))
                l_copies[-1].start()

    way = 1 - 2 * bit(0)
    beside, opposite = along_x(-way), along_x(2)

    sep_copies = [[] for _ in items]

    def sep_copy(i, where, sems, index, device):
        sep_copies[i].append(remote(where, where, sems, (i, index), device))
        sep_copies[i][-1].start()

    def sep_start(i):
        own_sep[i].wait()
        sep_copy(i, sep_buf.at[i, x], sep_sem, 0, to_x(way))

    def sep_forward(i):
        sep_copies[i][0].wait_recv()
        sep_copy(i, sep_buf.at[i, beside, pl.ds(bit(0) * BLOCK, BLOCK)], sep_sem, 1, to_x(way))
        sep_copy(i, sep_buf.at[i, beside], pass_sem, 0, across(0, 0))

    def sep_finish(i):
        sep_copies[i][1].wait_recv()
        sep_copy(i, sep_buf.at[i, opposite, pl.ds(bit(0) * BLOCK, BLOCK)], pass_sem, 1, across(0, 0))

    def sep_wait(i):
        sep_copies[i][2].wait_recv()
        sep_copies[i][3].wait_recv()

    for copy in mask_copies:
        copy.wait_recv()

    def weight(level, row_block):
        return jnp.where(owner_ref[node(level, 0)] == row_block * Z + z, 1.0, 0.0).astype(F32)

    core_copies = []
    y_copies = []
    order = [along_x(d) for d in (0, -1, 1, 2)]
    waits = [[], [2], [3], [4, 5]]
    giving = 1 - bit(1)
    total0 = [jnp.zeros((rows, BLOCK), F32) for _ in range(2)]
    for index in range(X + 1):
        if index < X:
            row_block = order[index]
            for which in waits[index]:
                l_copies[which].wait_recv()
            if index == X - 1:
                sep_start(0)
                sep_start(1)
            u_all = u_buf[...].reshape(panels * width, X * BLOCK)
            for r in range(rows // BLOCK):
                part = dot(l_buf[row_block, r * BLOCK : (r + 1) * BLOCK], u_all) * mask[row_block, r : r + 1]
                for h in range(2):
                    acc[h, row_block, r * BLOCK : (r + 1) * BLOCK] = part[:, h * 2 * BLOCK : (h + 1) * 2 * BLOCK]
            core_copies.append(
                remote(acc.at[1 - bit(0), row_block], other.at[row_block], core_sem, (index,), across(0, 0))
            )
            core_copies[-1].start()
        if index:
            row_block = order[index - 1]
            core_copies[index - 1].wait_recv()
            value = acc[bit(0), row_block] + other[row_block]
            for h in range(2):
                half[h, row_block] = value[:, h * BLOCK : (h + 1) * BLOCK]
                total0[h] = total0[h] + weight(0, row_block) * value[:, h * BLOCK : (h + 1) * BLOCK]
            give1[row_block] = half[giving, row_block].astype(BF16)
            y_copies.append(remote(give1.at[row_block], take1.at[row_block], y_sem, (index - 1,), across(1, 0)))
            y_copies[-1].start()

    late = []

    def each(low, act):
        for d in sorted(range(low, Z), key=lambda d: abs(d - Z // 2)):
            act(d)

    def part_copies(level, cand, parts):
        return lambda d: remote(cand.at[along_z(d)], parts.at[d], part_sem, (level, d), to_z(d))

    def add_parts(own, parts, copies):
        total = own.astype(F32)
        for d in range(1, Z):
            copies(d).wait_recv()
            total = total + parts[d].astype(F32)
        late.append((1, copies))
        return total

    def pivot_start(level, mine, theirs, pivot):
        def here(d):
            return remote(mine, pivot.at[0, z], pivot_sem, (level, d), to_z(d))

        def there(d):
            return remote(theirs, pivot.at[1, z], pivot_sem, (level, Z + d), across(level + 1, d))

        each(0, lambda d: there(d).start())
        each(1, lambda d: here(d).start())
        pivot[0, z] = mine[...]
        return here, there

    def pivot_wait(copies):
        here, there = copies
        each(1, lambda d: here(d).wait_recv())
        each(0, lambda d: there(d).wait_recv())
        late.extend([(1, here), (0, there)])

    def update(level, row_block, pivots):
        return sum(dot(sep_buf[2 * level + i, row_block], pivot) for i, pivot in enumerate(pivots))

    for h in range(2):
        cand0[:, h] = total0[h].astype(BF16).reshape(Z, rows // Z, BLOCK)
    copies = part_copies(0, cand0, parts0)
    each(1, lambda d: copies(d).start())
    for i in (0, 1):
        sep_forward(i)
    for i in (2, 3):
        sep_start(i)
    chunk0[...] = add_parts(cand0[z], parts0, copies).astype(BF16)
    for level in range(1, LEVELS):
        pl.semaphore_wait(ready_sem.at[level], 1)
    copies = pivot_start(0, chunk0.at[bit(1)], chunk0.at[giving], pivot0)
    for i in (0, 1):
        sep_finish(i)
    for i in (2, 3):
        sep_forward(i)
    for i in (4, 5, 6):
        sep_start(i)
    for i in (0, 1):
        sep_wait(i)
    pivot_wait(copies)

    picked = jnp.zeros((rows, BLOCK), F32)
    pivots = [pivot0[i].reshape(rows, BLOCK) for i in range(2)]
    for copy in y_copies:
        copy.wait_recv()
    for row_block in range(X):
        value = half[bit(1), row_block] - update(0, row_block, pivots)
        value = value + take1[row_block].astype(F32)
        state1[row_block] = value
        picked = picked + weight(1, row_block) * value
    cand1[...] = picked.astype(BF16).reshape(Z, rows // Z, BLOCK)
    copies = part_copies(1, cand1, parts1)
    each(1, lambda d: copies(d).start())

    def pack_two(blocks, store):
        pairs = len(blocks) // 2
        for pair in range(pairs):
            low, high = blocks[pair], blocks[pair + pairs]
            store[0, pair] = by_half(low, turned(high, 2))
            store[1, pair] = by_half(turned(low, 2), high)

    pack_two([state1[row_block] for row_block in range(X)], pack2)
    give2[...] = pack2[1 - bit(2)].astype(BF16)
    y_copies.append(remote(give2, take2, y_sem, (X,), across(2, 0)))
    y_copies[-1].start()
    for i in (2, 3):
        sep_finish(i)
    for i in (2, 3):
        sep_wait(i)
    block = sum(weight(2, row_block) * sep_buf[2 + bit(0), row_block].astype(F32) for row_block in range(X))
    for h in range(2):
        corner[:, h] = block[h * BLOCK : (h + 1) * BLOCK].astype(BF16).reshape(Z, rows // Z // 2, rows)

    def corner_copies(d):
        return remote(corner.at[along_z(d)], corner_parts.at[d], corner_sem, (0, d), to_z(d))

    each(1, lambda d: corner_copies(d).start())

    chunk1[...] = add_parts(cand1[z], parts1, copies).astype(BF16)
    pivot_copies = pivot_start(1, chunk1, chunk1, pivot1)
    for i in (4, 5, 6):
        sep_forward(i)

    y_copies[-1].wait_recv()
    value = pack2[bit(2)] + take2[...].astype(F32)
    state2[...] = value
    picked = by_half(*[weight(2, 2 * h) * value[0] + weight(2, 2 * h + 1) * value[1] for h in range(2)])
    picked = picked + turned(picked, 2)
    picked = by_half(picked[: rows // 2], picked[rows // 2 :])
    cand2[...] = picked.reshape(Z, rows // Z // 2, BLOCK)
    copies = part_copies(2, cand2, parts2)
    each(1, lambda d: copies(d).start())
    mine = corner_chunk.at[bit(0)]
    corner_chunk[bit(0)] = add_parts(corner[z], corner_parts, corner_copies).astype(BF16)
    corner_pass = remote(mine, mine, corner_pass_sem, (0,), across(0, 0))
    corner_pass.start()
    corner_pass.wait_recv()
    pivot_wait(pivot_copies)

    pivots = [pivot1[i].reshape(rows, BLOCK) for i in range(2)]
    taken = sum(dot(corner_chunk[i].reshape(rows // Z, rows), pivots[i]) for i in range(2))
    pack_two([taken[: rows // Z // 2], taken[rows // Z // 2 :]], pack_chunk)
    total = add_parts(cand2[z], parts2, copies)
    chunk2[...] = (total - pack_chunk[bit(2), 0]).astype(BF16)
    pivot_copies = pivot_start(2, chunk2, chunk2, pivot2)
    pack_two([update(1, row_block, pivots) for row_block in range(X)], pack2)
    state2[...] = state2[...] - pack2[bit(2)]

    def pack_four(even, odd):
        moved_even, moved_odd = turned(even, -1), turned(odd, 1)
        pack3[0] = by_group([even, moved_odd, even, moved_odd])
        pack3[1] = by_group([moved_even, odd, moved_even, odd])

    pack_four(state2[0], state2[1])
    give3[...] = pack3[1 - bit(3)].astype(BF16)
    y_copies.append(remote(give3, take3, y_sem, (X + 1,), across(3, 0)))
    y_copies[-1].start()
    for i in (4, 5, 6):
        sep_finish(i)
    for i in (4, 5, 6):
        sep_wait(i)
    pivot_wait(pivot_copies)

    pivots = []
    for i in range(2):
        packed = pivot2[i].astype(F32).reshape(rows // 2, BLOCK)
        moved = turned(packed, 2)
        pivots.append(jnp.concatenate([by_half(packed, moved), by_half(moved, packed)], axis=0).astype(BF16))
    updates = [update(2, row_block, pivots) for row_block in range(X)]
    pack_four(*[state2[pair] - by_half(updates[pair], updates[pair + 2]) for pair in range(2)])
    y_copies[-1].wait_recv()
    value = pack3[bit(3)] + take3[...].astype(F32)
    state3[...] = value
    picked = by_group([weight(3, g) * value for g in range(X)])
    picked = picked + turned(picked, 1)
    picked = picked + turned(picked, 2)
    quarter = rows // X
    cand3[...] = by_group([picked[k * quarter : (k + 1) * quarter] for k in range(X)]).astype(BF16)

    def whole_copies(d):
        return remote(cand3, parts3.at[d], part_sem, (3, d), to_z(d))

    each(1, lambda d: whole_copies(d).start())
    packed = add_parts(cand3[...], parts3, whole_copies)
    pivot = []
    for k in range(X):
        nothing = jnp.zeros_like(packed)
        one = by_group([packed if g == k else nothing for g in range(X)])
        one = one + turned(one, 1)
        pivot.append(one + turned(one, 2))
    pivot = jnp.concatenate(pivot, axis=0).astype(BF16)
    value = state3[...] - by_group([update(3, row_block, [pivot]) for row_block in range(X)])

    for row_block in range(X):
        slices[row_block] = by_group(
            [turned(value[k * quarter : (k + 1) * quarter], k - row_block) for k in range(X)]
        )
    final_copies = []
    for d in range(1, X):
        final_copies.append(remote(slices.at[along_x(d)], final.at[x], final_sem, (d - 1,), to_x(d)))
        final_copies[-1].start()
    final[x] = slices[x]
    for copy in final_copies:
        copy.wait_recv()
    for k in range(X):
        out_ref[k * quarter : (k + 1) * quarter, :] = by_group([turned(final[q], q - k) for q in range(X)])

    started = [corner_pass] + u_copies + mask_copies + l_copies + list(ring.values()) + core_copies + y_copies + final_copies
    for copy in started + [copy for item in sep_copies for copy in item]:
        copy.wait_send()
    for low, copies in late:
        each(low, lambda d, copies=copies: copies(d).wait_send())


def local(l_panels, u_panels, panel_fill, copy_fill, sep_panels, sep_owner):
    _, panels, rows, width = l_panels.shape
    depth, columns = u_panels.shape[2:]
    quarter = columns // X
    items = 2 * LEVELS - 1
    remote_sems = [
        (X - 1,), (X - 1,), (6,), (X * Z,), (X,), (items, 2), (items, 2), None, (X + 2,), (LEVELS, Z),
        (LEVELS - 1, 2 * Z), (X - 1,), (1, Z), (1,),
    ]
    chunk = rows // Z
    kept = pl.BlockSpec(memory_space=pl.ANY)
    return pl.pallas_call(
        kernel,
        out_shape=jax.ShapeDtypeStruct((rows, BLOCK), F32),
        in_specs=[kept] * 6,
        out_specs=pl.BlockSpec(memory_space=pltpu.VMEM),
        scratch_shapes=[
            pltpu.SMEM(sep_owner.shape, jnp.int32),
            pltpu.SMEM(panel_fill.shape, jnp.int32),
            pltpu.SMEM(copy_fill.shape, jnp.int32),
            pltpu.VMEM(l_panels.shape, BF16),
            pltpu.VMEM(u_panels.shape, BF16),
            pltpu.VMEM((X, panels, depth, quarter), BF16),
            pltpu.VMEM((panels, X, Z, depth, quarter), BF16),
            pltpu.VMEM((X, rows, panels * width), BF16),
            pltpu.VMEM((X, 8, quarter), F32),
            pltpu.VMEM((2, X, rows, 2 * BLOCK), F32),
            pltpu.VMEM((X, rows, 2 * BLOCK), F32),
            pltpu.VMEM((2, X, rows, BLOCK), F32),
            pltpu.VMEM((items, X, rows, sep_panels.shape[2]), BF16),
            pltpu.VMEM((X, rows, BLOCK), BF16),
            pltpu.VMEM((X, rows, BLOCK), BF16),
            pltpu.VMEM((X, rows, BLOCK), F32),
            pltpu.VMEM((2, 2, rows, BLOCK), F32),
            pltpu.VMEM((2, rows, BLOCK), BF16),
            pltpu.VMEM((2, rows, BLOCK), BF16),
            pltpu.VMEM((2, rows, BLOCK), F32),
            pltpu.VMEM((2, rows, BLOCK), F32),
            pltpu.VMEM((rows, BLOCK), BF16),
            pltpu.VMEM((rows, BLOCK), BF16),
            pltpu.VMEM((rows, BLOCK), F32),
            pltpu.VMEM((Z, 2, chunk, BLOCK), BF16),
            pltpu.VMEM((Z, 2, chunk, BLOCK), BF16),
            pltpu.VMEM((2, chunk, BLOCK), BF16),
            pltpu.VMEM((2, Z, chunk, BLOCK), BF16),
            pltpu.VMEM((Z, chunk, BLOCK), BF16),
            pltpu.VMEM((Z, chunk, BLOCK), BF16),
            pltpu.VMEM((chunk, BLOCK), BF16),
            pltpu.VMEM((2, Z, chunk, BLOCK), BF16),
            pltpu.VMEM((Z, chunk // 2, BLOCK), F32),
            pltpu.VMEM((Z, chunk // 2, BLOCK), F32),
            pltpu.VMEM((chunk // 2, BLOCK), BF16),
            pltpu.VMEM((2, Z, chunk // 2, BLOCK), BF16),
            pltpu.VMEM((rows // X, BLOCK), BF16),
            pltpu.VMEM((Z, rows // X, BLOCK), BF16),
            pltpu.VMEM((X, rows // X, BLOCK), F32),
            pltpu.VMEM((X, rows // X, BLOCK), F32),
            pltpu.VMEM((Z, 2, chunk // 2, rows), BF16),
            pltpu.VMEM((Z, 2, chunk // 2, rows), BF16),
            pltpu.VMEM((2, 2, chunk // 2, rows), BF16),
            pltpu.VMEM((2, 1, chunk // 2, BLOCK), F32),
            *[pltpu.SemaphoreType.DMA((items + 5,) if s is None else (2, *s)) for s in remote_sems],
            pltpu.SemaphoreType.REGULAR((LEVELS,)),
        ],
        compiler_params=pltpu.CompilerParams(
            collective_id=0, has_side_effects=True, vmem_limit_bytes=60 * 2**20
        ),
        cost_estimate=pl.CostEstimate(flops=2**31, bytes_accessed=2**22, transcendentals=0),
    )(sep_owner, panel_fill, copy_fill, l_panels, u_panels, sep_panels)


def solution(mesh):
    return jax.shard_map(
        local,
        mesh=mesh,
        in_specs=(
            P("layer", None, "grid", None),
            P("layer", None, "grid", None),
            P("layer", None, "grid", None),
            P("layer", "grid", None),
            P(None, "grid", None),
            P(),
        ),
        out_specs=P("grid", "layer"),
        check_vma=False,
    )
```
